32 devices in a mesh: rows: 32 (over z, y, x, core).
Axes of the slice: x: 2, y: 2, z: 4, core: 2. Of those that a mesh axis runs over, the one named last changes fastest.
Arguments:
- features: bfloat16 [32768, 1024], P('rows'), may hold values from -6 to 6
- flip_signs: int32 [32768], P('rows'), may hold values from -1 to 1, as said below
- sample_rows: int32 [4096], P('rows'), may hold values from 0 to 32767, as said below
Outputs:
- sketch: float32 [4096, 1024], P('rows')
- upper_factor: float32 [1024, 1024], replicated
- leverage: float32 [32768], P('rows')
The draws below stay inside these ranges and needn't reach their ends.
Inputs may be any that keep to these rules, and one draw needn't show every extreme that they name: `flip_signs`: every entry is -1 or 1. `sample_rows`: strictly increasing, with exactly 128 indices in each aligned block of 1024 rows; cut each such block into consecutive groups of 32 rows: every group holds at most max(1, 4) indices, and 128 / max(1, 4) groups of each block hold exactly that many.
All inputs are finite; a program needn't handle non-finite values.
Results may differ from the reference program's by a relative error of at most 0.004.
Values may be sent and summed in bfloat16 or wider, within the bound.
A program may use at most 128 MiB of HBM per device.

```python
import math
import jax
import jax.numpy as jnp
from jax import lax

COLS = 1024
FACTOR = 128
ROWS_DEV = 1024
SAMPLES = 4096
ROWS = 32768
N_ROWS = 32


def draw_flip_signs(key, part):
    return (2 * jax.random.randint(jax.random.fold_in(key, 11), (ROWS,), 0, 2) - 1).astype(jnp.int32)


def draw_sample_rows(key, part):
    blocks = ROWS // ROWS_DEV
    per_block = SAMPLES // blocks
    span = ROWS_DEV // blocks
    each = max(1, per_block // blocks)
    used = per_block // each
    slice_scores = jax.random.randint(jax.random.fold_in(key, 23), (blocks, blocks), 0, 1 << 14) * blocks
    slice_scores = slice_scores + jnp.arange(blocks, dtype=jnp.int32)[None, :]
    slices = jnp.sort(jnp.argsort(slice_scores, axis=1)[:, :used], axis=1).astype(jnp.int32)
    place_scores = jax.random.randint(jax.random.fold_in(key, 29), (blocks, used, span), 0, 1 << 14) * span
    place_scores = place_scores + jnp.arange(span, dtype=jnp.int32)[None, None, :]
    within = jnp.sort(jnp.argsort(place_scores, axis=2)[:, :, :each], axis=2).astype(jnp.int32)
    picked = slices[:, :, None] * span + within + (jnp.arange(blocks, dtype=jnp.int32) * ROWS_DEV)[:, None, None]
    return picked.reshape(-1).astype(jnp.int32)


def level_of(key, shape, cuts, low, high):
    def one(position, shards_of):
        heights = jax.random.uniform(jax.random.fold_in(jax.random.fold_in(key, 6), position), (shards_of,), jnp.float32, low / len(cuts), high / len(cuts))
        return jnp.repeat(jnp.exp(heights), shape[position] // shards_of).reshape((-1,) + (1,) * (len(shape) - position - 1))

    gain = one(*cuts[0])
    for cut in cuts[1:]:
        gain = gain * one(*cut)
    return gain


def normal_values(own_key, dims, scale, limit, pieces=(), kind=jnp.bfloat16):
    entries = jax.random.normal(own_key, dims, jnp.float32) * scale
    if len(pieces) > 0:
        entries = level_of(own_key, dims, pieces, -0.22, 0.18) * entries
    return jnp.clip(entries, min=-limit, max=limit).astype(kind)


def setup_inputs(seed: int = 0) -> dict:
    keys = jax.random.split(jax.random.key(seed), 4)
    features = normal_values(keys[0], (ROWS, COLS), 1.0, 6.0, ((0, 32),))
    flip_signs = draw_flip_signs(jax.random.fold_in(keys[3], 71), 0)
    sample_rows = draw_sample_rows(jax.random.fold_in(keys[3], 71), 0)
    return {"features": features, "flip_signs": flip_signs, "sample_rows": sample_rows}


def hadamard_table(dimension):
    positions = jnp.arange(dimension, dtype=jnp.int32)
    common_bits = positions[:, None] & positions[None, :]
    parity = jnp.zeros((dimension, dimension), jnp.int32)
    for bit_pos in range(max(dimension.bit_length() - 1, 0)):
        parity = parity + (common_bits >> bit_pos & 1)
    return (1 - 2 * (parity % 2)).astype(jnp.float32)

def local_transform(row_block, sign_rows):
    flipped = row_block * sign_rows.astype(jnp.bfloat16)[:, None]
    inner_table = hadamard_table(FACTOR)
    outer_table = hadamard_table(ROWS_DEV // FACTOR)
    grouped = flipped.reshape(ROWS_DEV // FACTOR, FACTOR, COLS).astype(jnp.float32)
    section_one = jnp.einsum('ka,bac->bkc', inner_table, grouped, precision=lax.Precision.HIGHEST).astype(jnp.bfloat16)
    section_two = jnp.einsum('jb,bkc->jkc', outer_table, section_one.astype(jnp.float32), precision=lax.Precision.HIGHEST).astype(jnp.bfloat16)
    return section_two.reshape(ROWS_DEV, COLS)

def reference(features, flip_signs, sample_rows):
    blocks = features.reshape(N_ROWS, ROWS_DEV, COLS)
    sign_blocks = flip_signs.reshape(N_ROWS, ROWS_DEV)
    mixed_rows = lax.map(lambda inputs_pair: local_transform(inputs_pair[0], inputs_pair[1]), (blocks, sign_blocks))
    owner_dev = (sample_rows // ROWS_DEV).astype(jnp.int32)
    local_rows = (sample_rows % ROWS_DEV).astype(jnp.int32)
    across = hadamard_table(N_ROWS)

    def accumulate(running, source_dev):
        taken_rows = lax.dynamic_index_in_dim(mixed_rows, source_dev, 0, keepdims=False)[local_rows]
        weight_col = across[owner_dev, source_dev]
        return (running + weight_col[:, None] * taken_rows.astype(jnp.float32), None)
    running, _ = lax.scan(accumulate, jnp.zeros((SAMPLES, COLS), jnp.float32), jnp.arange(N_ROWS, dtype=jnp.int32))
    sketch = running * (1.0 / math.sqrt(SAMPLES))
    gram_matrix = jnp.dot(sketch.T, sketch, precision=lax.Precision.HIGHEST)
    lower_factor = jnp.linalg.cholesky(gram_matrix)
    upper_factor = lower_factor.T

    def block_leverage(row_block):
        solved = jax.scipy.linalg.solve_triangular(lower_factor, row_block.astype(jnp.float32).T, lower=True)
        return lax.optimization_barrier(jnp.sum(solved * solved, axis=0)) * (ROWS_DEV * N_ROWS / COLS)
    leverage = lax.map(block_leverage, blocks).reshape(-1)
    return (sketch, upper_factor, leverage)
```

```python
import functools
import math

import jax
import jax.numpy as jnp
import numpy as np
from jax import lax
from jax.experimental import pallas as pl
from jax.experimental.pallas import tpu as pltpu
from jax.sharding import PartitionSpec as P

FACTOR = 128
SAMPLES = 4096
BLOCK = 128
PANEL = 16
F32 = jnp.float32
BF16 = jnp.bfloat16


def hadamard_array(dimension):
    table = np.ones((1, 1), np.float32)
    while table.shape[0] < dimension:
        table = np.block([[table, table], [table, -table]])
    return table


def halves(x):
    high = x.astype(BF16).astype(F32)
    return high, x - high


def dot3(a, b):
    a_high, a_low = halves(a)
    b_high, b_low = halves(b)
    left = jnp.concatenate([a_high, a_high, a_low], axis=1).astype(BF16)
    right = jnp.concatenate([b_high, b_low, b_high], axis=0).astype(BF16)
    return jnp.dot(left, right, preferred_element_type=F32)


def dot3_t(a, b):
    a_high, a_low = halves(a)
    b_high, b_low = halves(b)
    left = jnp.concatenate([a_high, a_high, a_low], axis=0).T.astype(BF16)
    right = jnp.concatenate([b_high, b_low, b_high], axis=0).astype(BF16)
    return jnp.dot(left, right, preferred_element_type=F32)


def transform_kernel(table_ref, signs_ref, features_ref, out_ref):
    groups = signs_ref.shape[0]
    table = table_ref[...]
    inner = []
    for b in range(groups):
        signed = (table * signs_ref[b : b + 1, :].astype(F32)).astype(BF16)
        rows = features_ref[b * FACTOR : (b + 1) * FACTOR, :]
        product = jnp.dot(signed, rows, preferred_element_type=F32)
        inner.append(product.astype(BF16).astype(F32))
    step = 1
    while step < groups:
        mixed = list(inner)
        for b in range(groups):
            if b & step == 0:
                mixed[b] = inner[b] + inner[b + step]
                mixed[b + step] = inner[b] - inner[b + step]
        inner = mixed
        step *= 2
    for b in range(groups):
        out_ref[b * FACTOR : (b + 1) * FACTOR, :] = inner[b].astype(BF16)


def transform(features, flip_signs):
    rows_dev, columns = features.shape
    tile = 128
    groups = rows_dev // FACTOR
    return pl.pallas_call(
        transform_kernel,
        grid=(columns // tile,),
        out_shape=jax.ShapeDtypeStruct((rows_dev, columns), BF16),
        in_specs=[
            pl.BlockSpec((FACTOR, FACTOR), lambda i: (0, 0)),
            pl.BlockSpec((groups, FACTOR), lambda i: (0, 0)),
            pl.BlockSpec((rows_dev, tile), lambda i: (0, i)),
        ],
        out_specs=pl.BlockSpec((rows_dev, tile), lambda i: (0, i)),
        compiler_params=pltpu.CompilerParams(vmem_limit_bytes=32 * 2**20),
        name="local_transform",
    )(jnp.asarray(hadamard_array(FACTOR)), flip_signs.reshape(groups, FACTOR), features)


def combine_kernel(most, span, rows_dev, position_ref, wanted_ref, received_ref, picked_ref, gram_ref):
    slots, samples = wanted_ref.shape
    total = received_ref.shape[0]
    position = position_ref[0]
    row_id = lax.broadcasted_iota(jnp.int32, (slots, samples), 0)
    inside = wanted_ref[...] - row_id // most * rows_dev - position * span
    mine = (inside >= 0) & (inside < span)
    earlier = (
        lax.broadcasted_iota(jnp.int32, (samples, samples), 0)
        < lax.broadcasted_iota(jnp.int32, (samples, samples), 1)
    )
    rank = jnp.dot(
        jnp.where(mine, 1.0, 0.0).astype(BF16),
        jnp.where(earlier, 1.0, 0.0).astype(BF16),
        preferred_element_type=F32,
    )
    hit = mine & (rank == (row_id % most).astype(F32))
    place = jnp.max(jnp.where(hit, inside, -1), axis=1, keepdims=True)
    to_block = lax.broadcasted_iota(jnp.int32, (slots, total), 0) // most
    column = lax.broadcasted_iota(jnp.int32, (slots, total), 1)
    bits = to_block & (column // span)
    shift = 16
    while shift >= 1:
        bits = bits ^ (bits >> shift)
        shift //= 2
    sign = (1 - 2 * (bits & 1)).astype(F32)
    choose = jnp.where(column % span == place, sign, 0.0).astype(BF16)
    picked = jnp.dot(choose, received_ref[...], preferred_element_type=F32)
    picked = picked * (1.0 / math.sqrt(SAMPLES))
    picked_ref[...] = picked
    high, low = halves(picked)
    left = jnp.concatenate([high, high, low], axis=0).T.astype(BF16)
    right = jnp.concatenate([high, low, high], axis=0).astype(BF16)
    columns = picked.shape[1]
    for start in range(0, columns, 256):
        gram_ref[start : start + 256, :] = jnp.dot(
            left[start : start + 256, :], right, preferred_element_type=F32
        )


def combine(wanted, received, position, most, span, rows_dev):
    slots = wanted.shape[0] * most
    columns = received.shape[1]
    repeated = jnp.repeat(wanted, most, axis=0)
    vmem = pl.BlockSpec(memory_space=pltpu.VMEM)
    return pl.pallas_call(
        functools.partial(combine_kernel, most, span, rows_dev),
        out_shape=(
            jax.ShapeDtypeStruct((slots, columns), F32),
            jax.ShapeDtypeStruct((columns, columns), F32),
        ),
        in_specs=[pl.BlockSpec(memory_space=pltpu.SMEM), vmem, vmem],
        out_specs=(vmem, vmem),
        compiler_params=pltpu.CompilerParams(vmem_limit_bytes=32 * 2**20),
        name="combine_pick_gram",
    )(position.reshape(1), repeated, received)


def factor_block(work_ref):
    row_id = lax.broadcasted_iota(jnp.int32, (PANEL, BLOCK), 0)
    for start in range(0, BLOCK, PANEL):
        left = work_ref[start : start + PANEL, :BLOCK]
        right = work_ref[start : start + PANEL, BLOCK:]
        cols = [
            jnp.broadcast_to(left[:, start + j : start + j + 1], (PANEL, BLOCK))
            for j in range(PANEL)
        ]
        for j in range(PANEL):
            root = lax.rsqrt(cols[j][j : j + 1, :])
            scaled = cols[j] * root
            for later in range(j + 1, PANEL):
                cols[later] = cols[later] - scaled * (cols[later][j : j + 1, :] * root)
            left_row = left[j : j + 1, :] * root
            right_row = right[j : j + 1, :] * root
            below = jnp.where(row_id > j, scaled, 0.0)
            left = jnp.where(row_id == j, left_row, left - below * left_row)
            right = jnp.where(row_id == j, right_row, right - below * right_row)
        work_ref[start : start + PANEL, :BLOCK] = left
        work_ref[start : start + PANEL, BLOCK:] = right
        rest = start + PANEL
        if rest < BLOCK:
            update = dot3_t(left, jnp.concatenate([left, right], axis=1))
            work_ref[rest:, :] = work_ref[rest:, :] - update[rest:, :]


def factor_kernel(gram_ref, features_ref, upper_ref, leverage_ref, state_ref, work_ref, right_ref):
    columns = gram_ref.shape[0]
    count = columns // BLOCK
    state_ref[...] = gram_ref[...]
    row_id = lax.broadcasted_iota(jnp.int32, (BLOCK, BLOCK), 0)
    col_id = lax.broadcasted_iota(jnp.int32, (BLOCK, BLOCK), 1)
    wide_id = lax.broadcasted_iota(jnp.int32, (BLOCK, columns), 1)

    def outer(k, carry):
        here = pl.multiple_of(k * BLOCK, BLOCK)
        rows = pl.ds(here, BLOCK)
        work_ref[:, :BLOCK] = state_ref[rows, rows]
        work_ref[:, BLOCK:] = jnp.where(row_id == col_id, 1.0, 0.0)
        factor_block(work_ref)
        inverse = jnp.where(col_id <= row_id, work_ref[:, BLOCK:], 0.0)
        panel = dot3(inverse, state_ref[rows, :])
        upper_ref[rows, :] = jnp.where(wide_id >= here + BLOCK, panel, 0.0)
        upper_ref[rows, rows] = jnp.where(col_id >= row_id, work_ref[:, :BLOCK], 0.0)
        state_ref[rows, :] = panel
        state_ref[rows, rows] = inverse
        high, low = halves(state_ref[rows, :])
        right_ref[...] = jnp.concatenate([high, low, high], axis=0).astype(BF16)

        def trailing(i, carry):
            below = pl.ds(pl.multiple_of(i * BLOCK, BLOCK), BLOCK)
            part = upper_ref[rows, below].T
            p_high, p_low = halves(part)
            left = jnp.concatenate([p_high, p_high, p_low], axis=1).astype(BF16)
            state_ref[below, rows] = jnp.zeros((BLOCK, BLOCK), F32)
            state_ref[below, :] = state_ref[below, :] - jnp.dot(
                left, right_ref[...], preferred_element_type=F32
            )
            return carry

        return lax.fori_loop(k + 1, count, trailing, carry)

    lax.fori_loop(0, count, outer, 0)
    total = jnp.zeros((1, features_ref.shape[0]), F32)
    tile = 2 * BLOCK
    for start in range(0, columns, tile):
        depth = start + tile
        block = state_ref[start:depth, :depth]
        keep = (
            lax.broadcasted_iota(jnp.int32, (tile, depth), 1)
            <= lax.broadcasted_iota(jnp.int32, (tile, depth), 0) + start
        )
        high, low = halves(jnp.where(keep, block, 0.0))
        stacked = jnp.concatenate([high, low], axis=0).astype(BF16)
        solved = lax.dot_general(
            stacked,
            features_ref[:, :depth],
            (((1,), (1,)), ((), ())),
            preferred_element_type=F32,
        )
        solved = solved[:tile] + solved[tile:]
        total = total + jnp.sum(solved * solved, axis=0, keepdims=True)
    leverage_ref[...] = total


def factor(gram, features):
    columns = gram.shape[0]
    rows_dev = features.shape[0]
    vmem = pl.BlockSpec(memory_space=pltpu.VMEM)
    return pl.pallas_call(
        factor_kernel,
        out_shape=(
            jax.ShapeDtypeStruct((columns, columns), F32),
            jax.ShapeDtypeStruct((1, rows_dev), F32),
        ),
        in_specs=[vmem, vmem],
        out_specs=(vmem, vmem),
        scratch_shapes=[
            pltpu.VMEM((columns, columns), F32),
            pltpu.VMEM((BLOCK, 2 * BLOCK), F32),
            pltpu.VMEM((3 * BLOCK, columns), BF16),
        ],
        compiler_params=pltpu.CompilerParams(vmem_limit_bytes=40 * 2**20),
        cost_estimate=pl.CostEstimate(
            flops=20 * columns**3, bytes_accessed=16 * columns**2, transcendentals=0
        ),
        name="cholesky_leverage",
    )(gram, features)


def rank_in_group(group_of):
    count = group_of.shape[-1]
    same = group_of[:, None] == group_of[None, :]
    order = jnp.arange(count, dtype=jnp.int32)
    before = order[:, None] < order[None, :]
    return jnp.sum((same & before).astype(jnp.int32), axis=0)


def shards(features, flip_signs, sample_rows):
    rows_dev, columns = features.shape
    group_size = lax.axis_size("rows")
    position = lax.axis_index("rows")
    span = rows_dev // group_size
    samp_dev = sample_rows.shape[0]
    most = max(1, samp_dev // group_size)
    wanted = lax.all_gather(sample_rows, "rows", axis=0, tiled=True).reshape(group_size, samp_dev)
    mixed_rows = transform(features, flip_signs)
    pieces = mixed_rows.reshape(group_size, span, columns)
    received = lax.all_to_all(pieces, "rows", split_axis=0, concat_axis=0, tiled=True)
    picked, partial = combine(
        wanted, received.reshape(rows_dev, columns), position, most, span, rows_dev
    )
    gram_matrix = lax.psum(partial, "rows")
    gram_matrix, picked = lax.optimization_barrier((gram_matrix, picked))
    returned = lax.all_to_all(
        picked.reshape(group_size, most, columns), "rows", split_axis=0, concat_axis=0, tiled=True
    )
    upper_factor, leverage = factor(gram_matrix, features)
    own_groups = (sample_rows - position * rows_dev) // span
    own_ranks = rank_in_group(own_groups)
    sketch = jnp.take(
        returned.reshape(group_size * most, columns), own_groups * most + own_ranks, axis=0
    )
    leverage = leverage.reshape(rows_dev) * (rows_dev * group_size / columns)
    return (sketch, upper_factor, leverage)


def solution(mesh):
    placed = (P("rows", None), P("rows"), P("rows"))
    return jax.shard_map(
        shards,
        mesh=mesh,
        in_specs=placed,
        out_specs=(P("rows", None), P(), P("rows")),
        check_vma=False,
    )
```

```python
import functools
import math

import jax
import jax.numpy as jnp
import numpy as np
from jax import lax
from jax.experimental import pallas as pl
from jax.experimental.pallas import tpu as pltpu
from jax.sharding import PartitionSpec as P

FACTOR = 128
SAMPLES = 4096
BLOCK = 128
PANEL = 16
F32 = jnp.float32
BF16 = jnp.bfloat16


def hadamard_array(dimension):
    table = np.ones((1, 1), np.float32)
    while table.shape[0] < dimension:
        table = np.block([[table, table], [table, -table]])
    return table


def halves(x):
    high = x.astype(BF16).astype(F32)
    return high, x - high


def dot3(a, b):
    a_high, a_low = halves(a)
    b_high, b_low = halves(b)
    left = jnp.concatenate([a_high, a_high, a_low], axis=1).astype(BF16)
    right = jnp.concatenate([b_high, b_low, b_high], axis=0).astype(BF16)
    return jnp.dot(left, right, preferred_element_type=F32)


def dot3_t(a, b):
    a_high, a_low = halves(a)
    b_high, b_low = halves(b)
    left = jnp.concatenate([a_high, a_high, a_low], axis=0).T.astype(BF16)
    right = jnp.concatenate([b_high, b_low, b_high], axis=0).astype(BF16)
    return jnp.dot(left, right, preferred_element_type=F32)


def transform_kernel(table_ref, signs_ref, features_ref, out_ref):
    groups = signs_ref.shape[0]
    table = table_ref[...]
    inner = []
    for b in range(groups):
        signed = (table * signs_ref[b : b + 1, :].astype(F32)).astype(BF16)
        rows = features_ref[b * FACTOR : (b + 1) * FACTOR, :]
        product = jnp.dot(signed, rows, preferred_element_type=F32)
        inner.append(product.astype(BF16).astype(F32))
    step = 1
    while step < groups:
        mixed = list(inner)
        for b in range(groups):
            if b & step == 0:
                mixed[b] = inner[b] + inner[b + step]
                mixed[b + step] = inner[b] - inner[b + step]
        inner = mixed
        step *= 2
    for b in range(groups):
        out_ref[b * FACTOR : (b + 1) * FACTOR, :] = inner[b].astype(BF16)


def transform(features, flip_signs):
    rows_dev, columns = features.shape
    tile = 128
    groups = rows_dev // FACTOR
    return pl.pallas_call(
        transform_kernel,
        grid=(columns // tile,),
        out_shape=jax.ShapeDtypeStruct((rows_dev, columns), BF16),
        in_specs=[
            pl.BlockSpec((FACTOR, FACTOR), lambda i: (0, 0)),
            pl.BlockSpec((groups, FACTOR), lambda i: (0, 0)),
            pl.BlockSpec((rows_dev, tile), lambda i: (0, i)),
        ],
        out_specs=pl.BlockSpec((rows_dev, tile), lambda i: (0, i)),
        compiler_params=pltpu.CompilerParams(vmem_limit_bytes=32 * 2**20),
        name="local_transform",
    )(jnp.asarray(hadamard_array(FACTOR)), flip_signs.reshape(groups, FACTOR), features)


def combine_kernel(most, span, rows_dev, position_ref, wanted_ref, received_ref, picked_ref, rounded_ref):
    slots, samples = wanted_ref.shape
    total = received_ref.shape[0]
    position = position_ref[0]
    row_id = lax.broadcasted_iota(jnp.int32, (slots, samples), 0)
    inside = wanted_ref[...] - row_id // most * rows_dev - position * span
    mine = (inside >= 0) & (inside < span)
    earlier = (
        lax.broadcasted_iota(jnp.int32, (samples, samples), 0)
        < lax.broadcasted_iota(jnp.int32, (samples, samples), 1)
    )
    rank = jnp.dot(
        jnp.where(mine, 1.0, 0.0).astype(BF16),
        jnp.where(earlier, 1.0, 0.0).astype(BF16),
        preferred_element_type=F32,
    )
    hit = mine & (rank == (row_id % most).astype(F32))
    place = jnp.max(jnp.where(hit, inside, -1), axis=1, keepdims=True)
    to_block = lax.broadcasted_iota(jnp.int32, (slots, total), 0) // most
    column = lax.broadcasted_iota(jnp.int32, (slots, total), 1)
    bits = to_block & (column // span)
    shift = 16
    while shift >= 1:
        bits = bits ^ (bits >> shift)
        shift //= 2
    sign = (1 - 2 * (bits & 1)).astype(F32)
    choose = jnp.where(column % span == place, sign, 0.0).astype(BF16)
    picked = jnp.dot(choose, received_ref[...], preferred_element_type=F32)
    picked = picked * (1.0 / math.sqrt(SAMPLES))
    picked_ref[...] = picked
    rounded_ref[...] = picked.astype(BF16)


def combine(wanted, received, position, most, span, rows_dev):
    slots = wanted.shape[0] * most
    columns = received.shape[1]
    repeated = jnp.repeat(wanted, most, axis=0)
    vmem = pl.BlockSpec(memory_space=pltpu.VMEM)
    return pl.pallas_call(
        functools.partial(combine_kernel, most, span, rows_dev),
        out_shape=(
            jax.ShapeDtypeStruct((slots, columns), F32),
            jax.ShapeDtypeStruct((slots, columns), BF16),
        ),
        in_specs=[pl.BlockSpec(memory_space=pltpu.SMEM), vmem, vmem],
        out_specs=(vmem, vmem),
        compiler_params=pltpu.CompilerParams(vmem_limit_bytes=32 * 2**20),
        name="combine_pick",
    )(position.reshape(1), repeated, received)


def factor_block(work_ref):
    row_id = lax.broadcasted_iota(jnp.int32, (PANEL, BLOCK), 0)
    for start in range(0, BLOCK, PANEL):
        left = work_ref[start : start + PANEL, :BLOCK]
        right = work_ref[start : start + PANEL, BLOCK:]
        cols = [
            jnp.broadcast_to(left[:, start + j : start + j + 1], (PANEL, BLOCK))
            for j in range(PANEL)
        ]
        for j in range(PANEL):
            root = lax.rsqrt(cols[j][j : j + 1, :])
            scaled = cols[j] * root
            for later in range(j + 1, PANEL):
                cols[later] = cols[later] - scaled * (cols[later][j : j + 1, :] * root)
            left_row = left[j : j + 1, :] * root
            right_row = right[j : j + 1, :] * root
            below = jnp.where(row_id > j, scaled, 0.0)
            left = jnp.where(row_id == j, left_row, left - below * left_row)
            right = jnp.where(row_id == j, right_row, right - below * right_row)
        work_ref[start : start + PANEL, :BLOCK] = left
        work_ref[start : start + PANEL, BLOCK:] = right
        rest = start + PANEL
        if rest < BLOCK:
            update = dot3_t(left, jnp.concatenate([left, right], axis=1))
            work_ref[rest:, :] = work_ref[rest:, :] - update[rest:, :]


def factor_kernel(gram_ref, features_ref, upper_ref, leverage_ref, state_ref, work_ref, right_ref):
    columns = gram_ref.shape[0]
    count = columns // BLOCK
    state_ref[...] = gram_ref[...]
    row_id = lax.broadcasted_iota(jnp.int32, (BLOCK, BLOCK), 0)
    col_id = lax.broadcasted_iota(jnp.int32, (BLOCK, BLOCK), 1)
    wide_id = lax.broadcasted_iota(jnp.int32, (BLOCK, columns), 1)

    def outer(k, carry):
        here = pl.multiple_of(k * BLOCK, BLOCK)
        rows = pl.ds(here, BLOCK)
        work_ref[:, :BLOCK] = state_ref[rows, rows]
        work_ref[:, BLOCK:] = jnp.where(row_id == col_id, 1.0, 0.0)
        factor_block(work_ref)
        inverse = jnp.where(col_id <= row_id, work_ref[:, BLOCK:], 0.0)
        panel = dot3(inverse, state_ref[rows, :])
        upper_ref[rows, :] = jnp.where(wide_id >= here + BLOCK, panel, 0.0)
        upper_ref[rows, rows] = jnp.where(col_id >= row_id, work_ref[:, :BLOCK], 0.0)
        state_ref[rows, :] = panel
        state_ref[rows, rows] = inverse
        high, low = halves(state_ref[rows, :])
        right_ref[...] = jnp.concatenate([high, low, high], axis=0).astype(BF16)

        def trailing(i, carry):
            below = pl.ds(pl.multiple_of(i * BLOCK, BLOCK), BLOCK)
            part = upper_ref[rows, below].T
            p_high, p_low = halves(part)
            left = jnp.concatenate([p_high, p_high, p_low], axis=1).astype(BF16)
            state_ref[below, rows] = jnp.zeros((BLOCK, BLOCK), F32)
            state_ref[below, :] = state_ref[below, :] - jnp.dot(
                left, right_ref[...], preferred_element_type=F32
            )
            return carry

        return lax.fori_loop(k + 1, count, trailing, carry)

    lax.fori_loop(0, count, outer, 0)
    total = jnp.zeros((1, features_ref.shape[0]), F32)
    tile = 2 * BLOCK
    for start in range(0, columns, tile):
        depth = start + tile
        block = state_ref[start:depth, :depth]
        keep = (
            lax.broadcasted_iota(jnp.int32, (tile, depth), 1)
            <= lax.broadcasted_iota(jnp.int32, (tile, depth), 0) + start
        )
        high, low = halves(jnp.where(keep, block, 0.0))
        stacked = jnp.concatenate([high, low], axis=0).astype(BF16)
        solved = lax.dot_general(
            stacked,
            features_ref[:, :depth],
            (((1,), (1,)), ((), ())),
            preferred_element_type=F32,
        )
        solved = solved[:tile] + solved[tile:]
        total = total + jnp.sum(solved * solved, axis=0, keepdims=True)
    leverage_ref[...] = total


def factor(gram, features):
    columns = gram.shape[0]
    rows_dev = features.shape[0]
    vmem = pl.BlockSpec(memory_space=pltpu.VMEM)
    return pl.pallas_call(
        factor_kernel,
        out_shape=(
            jax.ShapeDtypeStruct((columns, columns), F32),
            jax.ShapeDtypeStruct((1, rows_dev), F32),
        ),
        in_specs=[vmem, vmem],
        out_specs=(vmem, vmem),
        scratch_shapes=[
            pltpu.VMEM((columns, columns), F32),
            pltpu.VMEM((BLOCK, 2 * BLOCK), F32),
            pltpu.VMEM((3 * BLOCK, columns), BF16),
        ],
        compiler_params=pltpu.CompilerParams(vmem_limit_bytes=40 * 2**20),
        cost_estimate=pl.CostEstimate(
            flops=20 * columns**3, bytes_accessed=16 * columns**2, transcendentals=0
        ),
        name="cholesky_leverage",
    )(gram, features)


def rank_in_group(group_of):
    count = group_of.shape[-1]
    same = group_of[:, None] == group_of[None, :]
    order = jnp.arange(count, dtype=jnp.int32)
    before = order[:, None] < order[None, :]
    return jnp.sum((same & before).astype(jnp.int32), axis=0)


def shards(features, flip_signs, sample_rows):
    rows_dev, columns = features.shape
    group_size = lax.axis_size("rows")
    position = lax.axis_index("rows")
    span = rows_dev // group_size
    samp_dev = sample_rows.shape[0]
    most = max(1, samp_dev // group_size)
    wanted = lax.all_gather(sample_rows, "rows", axis=0, tiled=True).reshape(group_size, samp_dev)
    wanted, flip_signs = lax.optimization_barrier((wanted, flip_signs))
    mixed_rows = transform(features, flip_signs)
    pieces = mixed_rows.reshape(group_size, span, columns)
    received = lax.all_to_all(pieces, "rows", split_axis=0, concat_axis=0, tiled=True)
    picked, rounded = combine(
        wanted, received.reshape(rows_dev, columns), position, most, span, rows_dev
    )
    everything = lax.all_gather(rounded, "rows", axis=0, tiled=True)
    gram_matrix = lax.dot_general(
        everything, everything, (((0,), (0,)), ((), ())), preferred_element_type=F32
    )
    gram_matrix, picked = lax.optimization_barrier((gram_matrix, picked))
    returned = lax.all_to_all(
        picked.reshape(group_size, most, columns), "rows", split_axis=0, concat_axis=0, tiled=True
    )
    upper_factor, leverage = factor(gram_matrix, features)
    own_groups = (sample_rows - position * rows_dev) // span
    own_ranks = rank_in_group(own_groups)
    sketch = jnp.take(
        returned.reshape(group_size * most, columns), own_groups * most + own_ranks, axis=0
    )
    leverage = leverage.reshape(rows_dev) * (rows_dev * group_size / columns)
    return (sketch, upper_factor, leverage)


def solution(mesh):
    placed = (P("rows", None), P("rows"), P("rows"))
    return jax.shard_map(
        shards,
        mesh=mesh,
        in_specs=placed,
        out_specs=(P("rows", None), P(), P("rows")),
        check_vma=False,
    )
```

```python
import functools
import math

import jax
import jax.numpy as jnp
import numpy as np
from jax import lax
from jax.experimental import pallas as pl
from jax.experimental.pallas import tpu as pltpu
from jax.sharding import PartitionSpec as P

FACTOR = 128
SAMPLES = 4096
BLOCK = 128
PANEL = 16
F32 = jnp.float32
BF16 = jnp.bfloat16


def hadamard_array(dimension):
    table = np.ones((1, 1), np.float32)
    while table.shape[0] < dimension:
        table = np.block([[table, table], [table, -table]])
    return table


def halves(x):
    high = x.astype(BF16).astype(F32)
    return high, x - high


def dot3(a, b):
    a_high, a_low = halves(a)
    b_high, b_low = halves(b)
    left = jnp.concatenate([a_high, a_high, a_low], axis=1).astype(BF16)
    right = jnp.concatenate([b_high, b_low, b_high], axis=0).astype(BF16)
    return jnp.dot(left, right, preferred_element_type=F32)


def dot3_t(a, b):
    a_high, a_low = halves(a)
    b_high, b_low = halves(b)
    left = jnp.concatenate([a_high, a_high, a_low], axis=0).T.astype(BF16)
    right = jnp.concatenate([b_high, b_low, b_high], axis=0).astype(BF16)
    return jnp.dot(left, right, preferred_element_type=F32)


def transform_kernel(table_ref, signs_ref, features_ref, out_ref):
    groups = signs_ref.shape[0]
    table = table_ref[...]
    inner = []
    for b in range(groups):
        signed = (table * signs_ref[b : b + 1, :].astype(F32)).astype(BF16)
        rows = features_ref[b * FACTOR : (b + 1) * FACTOR, :]
        product = jnp.dot(signed, rows, preferred_element_type=F32)
        inner.append(product.astype(BF16).astype(F32))
    step = 1
    while step < groups:
        mixed = list(inner)
        for b in range(groups):
            if b & step == 0:
                mixed[b] = inner[b] + inner[b + step]
                mixed[b + step] = inner[b] - inner[b + step]
        inner = mixed
        step *= 2
    for b in range(groups):
        out_ref[b * FACTOR : (b + 1) * FACTOR, :] = inner[b].astype(BF16)


def transform(features, flip_signs):
    rows_dev, columns = features.shape
    tile = 128
    groups = rows_dev // FACTOR
    return pl.pallas_call(
        transform_kernel,
        grid=(columns // tile,),
        out_shape=jax.ShapeDtypeStruct((rows_dev, columns), BF16),
        in_specs=[
            pl.BlockSpec((FACTOR, FACTOR), lambda i: (0, 0)),
            pl.BlockSpec((groups, FACTOR), lambda i: (0, 0)),
            pl.BlockSpec((rows_dev, tile), lambda i: (0, i)),
        ],
        out_specs=pl.BlockSpec((rows_dev, tile), lambda i: (0, i)),
        compiler_params=pltpu.CompilerParams(vmem_limit_bytes=32 * 2**20),
        name="local_transform",
    )(jnp.asarray(hadamard_array(FACTOR)), flip_signs.reshape(groups, FACTOR), features)


def place_of(device):
    return {"rows": device}


def greet(partners):
    barrier = pltpu.get_barrier_semaphore()
    for partner in partners:
        pl.semaphore_signal(
            barrier, inc=1, device_id=place_of(partner), device_id_type=pl.DeviceIdType.MESH
        )
    pl.semaphore_wait(barrier, len(partners))


def exchange_kernel(pieces_ref, rows_ref, received_ref, wanted_ref, send, recv, row_send, row_recv):
    size = pieces_ref.shape[0]
    me = lax.axis_index("rows")
    barrier = pltpu.get_barrier_semaphore()

    def signal(offset, carry):
        pl.semaphore_signal(
            barrier,
            inc=1,
            device_id=place_of(lax.rem(me + offset, size)),
            device_id_type=pl.DeviceIdType.MESH,
        )
        return carry

    lax.fori_loop(1, size, signal, 0)
    pl.semaphore_wait(barrier, size - 1)

    def copies(step):
        offset = 1 + lax.rem(size // 2 - 1 + step, size - 1)
        partner = lax.rem(me + offset, size)
        rows = pltpu.make_async_remote_copy(
            src_ref=rows_ref.at[0],
            dst_ref=wanted_ref.at[me],
            send_sem=row_send.at[offset],
            recv_sem=row_recv.at[offset],
            device_id=place_of(partner),
            device_id_type=pl.DeviceIdType.MESH,
        )
        data = pltpu.make_async_remote_copy(
            src_ref=pieces_ref.at[partner],
            dst_ref=received_ref.at[me],
            send_sem=send.at[offset],
            recv_sem=recv.at[offset],
            device_id=place_of(partner),
            device_id_type=pl.DeviceIdType.MESH,
        )
        return rows, data

    def begin(step, carry):
        for copy in copies(step):
            copy.start()
        return carry

    lax.fori_loop(0, size - 1, begin, 0)
    received_ref[me] = pieces_ref[me]
    wanted_ref[me] = rows_ref[0]

    def finish(step, carry):
        for copy in copies(step):
            copy.wait()
        return carry

    lax.fori_loop(0, size - 1, finish, 0)


def exchange(pieces, sample_rows):
    size = pieces.shape[0]
    samples = sample_rows.shape[0]
    vmem = pl.BlockSpec(memory_space=pltpu.VMEM)
    received, wanted = pl.pallas_call(
        exchange_kernel,
        out_shape=(
            jax.ShapeDtypeStruct(pieces.shape, pieces.dtype),
            jax.ShapeDtypeStruct((size, 1, samples), jnp.int32),
        ),
        in_specs=[vmem, vmem],
        out_specs=(vmem, vmem),
        scratch_shapes=[pltpu.SemaphoreType.DMA((size,))] * 4,
        compiler_params=pltpu.CompilerParams(
            collective_id=1, has_side_effects=True, vmem_limit_bytes=24 * 2**20
        ),
        name="exchange_rows",
    )(pieces, sample_rows.reshape(1, 1, samples))
    return received, wanted.reshape(size, samples)


def sum_kernel(orders, packed_ref, gram_ref, work, land, summed, send, recv):
    me = lax.axis_index("rows")
    stages = len(orders[0])
    span = packed_ref.shape[0] // len(orders)
    bit = [me // 2**b % 2 for b in range(stages)]
    partner = [me + (1 - 2 * bit[b]) * 2**b for b in range(stages)]
    greet(partner)

    def rows(start, size):
        return pl.ds(pl.multiple_of(start, 8), size)

    def reduce_part(part, order):
        start, size, landing = part * span, span, part * span
        kept = []
        for stage, b in enumerate(order):
            size //= 2
            source = packed_ref if stage == 0 else work
            kept_start = start + bit[b] * size
            copy = pltpu.make_async_remote_copy(
                src_ref=source.at[rows(start + (1 - bit[b]) * size, size), :],
                dst_ref=land.at[pl.ds(landing, size), :],
                send_sem=send.at[part, stage],
                recv_sem=recv.at[part, stage],
                device_id=place_of(partner[b]),
                device_id_type=pl.DeviceIdType.MESH,
            )
            copy.start()
            yield
            copy.wait()
            target = work if stage < stages - 1 else summed
            target[rows(kept_start, size), :] = (
                source[rows(kept_start, size), :] + land[pl.ds(landing, size), :]
            )
            landing += size
            start = kept_start
            kept.append((b, start, size))
        for stage, (b, start, size) in enumerate(reversed(kept)):
            block = summed.at[rows(start, size), :]
            copy = pltpu.make_async_remote_copy(
                src_ref=block,
                dst_ref=block,
                send_sem=send.at[part, stages + stage],
                recv_sem=recv.at[part, stages + stage],
                device_id=place_of(partner[b]),
                device_id_type=pl.DeviceIdType.MESH,
            )
            copy.start()
            yield
            copy.wait()

    parts = [reduce_part(part, order) for part, order in enumerate(orders)]
    done = object()
    while parts:
        parts = [part for part in parts if next(part, done) is not done]
    unpack(summed, gram_ref)


def blocks_of(columns):
    count = columns // BLOCK
    for i in range(count // 2):
        yield i, i, 0
        yield count - 1 - i, i, (count - i) * BLOCK


def unpack(packed_ref, gram_ref):
    columns = gram_ref.shape[0]
    for block, row, at in blocks_of(columns):
        width = columns - block * BLOCK
        gram_ref[block * BLOCK : (block + 1) * BLOCK, block * BLOCK :] = packed_ref[
            row * BLOCK : (row + 1) * BLOCK, at : at + width
        ]
        if block:
            gram_ref[block * BLOCK : (block + 1) * BLOCK, : block * BLOCK] = jnp.zeros(
                (BLOCK, block * BLOCK), F32
            )


def sum_over_devices(packed, size):
    rows, width = packed.shape
    columns = 2 * rows
    vmem = pl.BlockSpec(memory_space=pltpu.VMEM)
    bits = list(range(size.bit_length() - 1))
    other = list(bits)
    other[1], other[2] = bits[2], bits[1]
    return pl.pallas_call(
        functools.partial(sum_kernel, (bits, other)),
        out_shape=jax.ShapeDtypeStruct((columns, columns), F32),
        in_specs=[vmem],
        out_specs=vmem,
        scratch_shapes=[
            pltpu.VMEM((rows, width), F32),
            pltpu.VMEM((rows, width), F32),
            pltpu.VMEM((rows, width), F32),
            pltpu.SemaphoreType.DMA((2, 2 * len(bits))),
            pltpu.SemaphoreType.DMA((2, 2 * len(bits))),
        ],
        compiler_params=pltpu.CompilerParams(
            collective_id=2, has_side_effects=True, vmem_limit_bytes=24 * 2**20
        ),
        name="sum_grams",
    )(packed)


def unpack_whole(packed):
    columns = 2 * packed.shape[0]
    gram = jnp.zeros((columns, columns), F32)
    for block, row, at in blocks_of(columns):
        width = columns - block * BLOCK
        part = packed[row * BLOCK : (row + 1) * BLOCK, at : at + width]
        gram = lax.dynamic_update_slice(gram, part, (block * BLOCK, block * BLOCK))
    return gram


def combine_kernel(most, span, rows_dev, position_ref, wanted_ref, received_ref, picked_ref, packed_ref):
    slots, samples = wanted_ref.shape
    total = received_ref.shape[0]
    position = position_ref[0]
    row_id = lax.broadcasted_iota(jnp.int32, (slots, samples), 0)
    inside = wanted_ref[...] - row_id // most * rows_dev - position * span
    mine = (inside >= 0) & (inside < span)
    earlier = (
        lax.broadcasted_iota(jnp.int32, (samples, samples), 0)
        < lax.broadcasted_iota(jnp.int32, (samples, samples), 1)
    )
    rank = jnp.dot(
        jnp.where(mine, 1.0, 0.0).astype(BF16),
        jnp.where(earlier, 1.0, 0.0).astype(BF16),
        preferred_element_type=F32,
    )
    hit = mine & (rank == (row_id % most).astype(F32))
    place = jnp.max(jnp.where(hit, inside, -1), axis=1, keepdims=True)
    to_block = lax.broadcasted_iota(jnp.int32, (slots, total), 0) // most
    column = lax.broadcasted_iota(jnp.int32, (slots, total), 1)
    bits = to_block & (column // span)
    shift = 16
    while shift >= 1:
        bits = bits ^ (bits >> shift)
        shift //= 2
    sign = (1 - 2 * (bits & 1)).astype(F32)
    choose = jnp.where(column % span == place, sign, 0.0).astype(BF16)
    picked = jnp.dot(choose, received_ref[...], preferred_element_type=F32)
    picked = picked * (1.0 / math.sqrt(SAMPLES))
    picked_ref[...] = picked
    high, low = halves(picked)
    left = jnp.concatenate([high, high, low], axis=0).T.astype(BF16)
    right = jnp.concatenate([high, low, high], axis=0).astype(BF16)
    columns = picked.shape[1]
    for block, row, at in blocks_of(columns):
        start = block * BLOCK
        packed_ref[row * BLOCK : (row + 1) * BLOCK, at : at + columns - start] = jnp.dot(
            left[start : start + BLOCK, :], right[:, start:], preferred_element_type=F32
        )


def combine(wanted, received, position, most, span, rows_dev):
    slots = wanted.shape[0] * most
    columns = received.shape[1]
    repeated = jnp.repeat(wanted, most, axis=0)
    vmem = pl.BlockSpec(memory_space=pltpu.VMEM)
    return pl.pallas_call(
        functools.partial(combine_kernel, most, span, rows_dev),
        out_shape=(
            jax.ShapeDtypeStruct((slots, columns), F32),
            jax.ShapeDtypeStruct((columns // 2, columns + BLOCK), F32),
        ),
        in_specs=[pl.BlockSpec(memory_space=pltpu.SMEM), vmem, vmem],
        out_specs=(vmem, vmem),
        compiler_params=pltpu.CompilerParams(vmem_limit_bytes=32 * 2**20),
        name="combine_pick_gram",
    )(position.reshape(1), repeated, received)


def factor_block(work_ref):
    row_id = lax.broadcasted_iota(jnp.int32, (PANEL, BLOCK), 0)
    for start in range(0, BLOCK, PANEL):
        left = work_ref[start : start + PANEL, :BLOCK]
        right = work_ref[start : start + PANEL, BLOCK:]
        cols = [
            jnp.broadcast_to(left[:, start + j : start + j + 1], (PANEL, BLOCK))
            for j in range(PANEL)
        ]
        for j in range(PANEL):
            root = lax.rsqrt(cols[j][j : j + 1, :])
            scaled = cols[j] * root
            for later in range(j + 1, PANEL):
                cols[later] = cols[later] - scaled * (cols[later][j : j + 1, :] * root)
            left_row = left[j : j + 1, :] * root
            right_row = right[j : j + 1, :] * root
            below = jnp.where(row_id > j, scaled, 0.0)
            left = jnp.where(row_id == j, left_row, left - below * left_row)
            right = jnp.where(row_id == j, right_row, right - below * right_row)
        work_ref[start : start + PANEL, :BLOCK] = left
        work_ref[start : start + PANEL, BLOCK:] = right
        rest = start + PANEL
        if rest < BLOCK:
            update = dot3_t(left, jnp.concatenate([left, right], axis=1))
            work_ref[rest:, :] = work_ref[rest:, :] - update[rest:, :]


def factor_kernel(gram_ref, features_ref, upper_ref, leverage_ref, state_ref, work_ref, right_ref):
    columns = gram_ref.shape[0]
    count = columns // BLOCK
    state_ref[...] = gram_ref[...]
    row_id = lax.broadcasted_iota(jnp.int32, (BLOCK, BLOCK), 0)
    col_id = lax.broadcasted_iota(jnp.int32, (BLOCK, BLOCK), 1)
    wide_id = lax.broadcasted_iota(jnp.int32, (BLOCK, columns), 1)

    def outer(k, carry):
        here = pl.multiple_of(k * BLOCK, BLOCK)
        rows = pl.ds(here, BLOCK)
        work_ref[:, :BLOCK] = state_ref[rows, rows]
        work_ref[:, BLOCK:] = jnp.where(row_id == col_id, 1.0, 0.0)
        factor_block(work_ref)
        inverse = jnp.where(col_id <= row_id, work_ref[:, BLOCK:], 0.0)
        panel = dot3(inverse, state_ref[rows, :])
        upper_ref[rows, :] = jnp.where(wide_id >= here + BLOCK, panel, 0.0)
        upper_ref[rows, rows] = jnp.where(col_id >= row_id, work_ref[:, :BLOCK], 0.0)
        state_ref[rows, :] = panel
        state_ref[rows, rows] = inverse
        high, low = halves(state_ref[rows, :])
        right_ref[...] = jnp.concatenate([high, low, high], axis=0).astype(BF16)

        def trailing(i, carry):
            below = pl.ds(pl.multiple_of(i * BLOCK, BLOCK), BLOCK)
            part = upper_ref[rows, below].T
            p_high, p_low = halves(part)
            left = jnp.concatenate([p_high, p_high, p_low], axis=1).astype(BF16)
            state_ref[below, rows] = jnp.zeros((BLOCK, BLOCK), F32)
            state_ref[below, :] = state_ref[below, :] - jnp.dot(
                left, right_ref[...], preferred_element_type=F32
            )
            return carry

        return lax.fori_loop(k + 1, count, trailing, carry)

    lax.fori_loop(0, count, outer, 0)
    total = jnp.zeros((1, features_ref.shape[0]), F32)
    tile = 2 * BLOCK
    for start in range(0, columns, tile):
        depth = start + tile
        block = state_ref[start:depth, :depth]
        keep = (
            lax.broadcasted_iota(jnp.int32, (tile, depth), 1)
            <= lax.broadcasted_iota(jnp.int32, (tile, depth), 0) + start
        )
        high, low = halves(jnp.where(keep, block, 0.0))
        stacked = jnp.concatenate([high, low], axis=0).astype(BF16)
        solved = lax.dot_general(
            stacked,
            features_ref[:, :depth],
            (((1,), (1,)), ((), ())),
            preferred_element_type=F32,
        )
        solved = solved[:tile] + solved[tile:]
        total = total + jnp.sum(solved * solved, axis=0, keepdims=True)
    leverage_ref[...] = total


def factor(gram, features):
    columns = gram.shape[0]
    rows_dev = features.shape[0]
    vmem = pl.BlockSpec(memory_space=pltpu.VMEM)
    return pl.pallas_call(
        factor_kernel,
        out_shape=(
            jax.ShapeDtypeStruct((columns, columns), F32),
            jax.ShapeDtypeStruct((1, rows_dev), F32),
        ),
        in_specs=[vmem, vmem],
        out_specs=(vmem, vmem),
        scratch_shapes=[
            pltpu.VMEM((columns, columns), F32),
            pltpu.VMEM((BLOCK, 2 * BLOCK), F32),
            pltpu.VMEM((3 * BLOCK, columns), BF16),
        ],
        compiler_params=pltpu.CompilerParams(vmem_limit_bytes=40 * 2**20),
        cost_estimate=pl.CostEstimate(
            flops=20 * columns**3, bytes_accessed=16 * columns**2, transcendentals=0
        ),
        name="cholesky_leverage",
    )(gram, features)


def rank_in_group(group_of):
    count = group_of.shape[-1]
    same = group_of[:, None] == group_of[None, :]
    order = jnp.arange(count, dtype=jnp.int32)
    before = order[:, None] < order[None, :]
    return jnp.sum((same & before).astype(jnp.int32), axis=0)


def shards(features, flip_signs, sample_rows):
    rows_dev, columns = features.shape
    group_size = lax.axis_size("rows")
    position = lax.axis_index("rows")
    span = rows_dev // group_size
    samp_dev = sample_rows.shape[0]
    most = max(1, samp_dev // group_size)
    pieces = transform(features, flip_signs).reshape(group_size, span, columns)
    if span % 16 == 0:
        received, wanted = exchange(pieces, sample_rows)
    else:
        wanted = lax.all_gather(sample_rows, "rows", axis=0, tiled=True)
        wanted = wanted.reshape(group_size, samp_dev)
        received = lax.all_to_all(pieces, "rows", split_axis=0, concat_axis=0, tiled=True)
    picked, packed = combine(
        wanted, received.reshape(rows_dev, columns), position, most, span, rows_dev
    )
    if 4 < group_size and columns // 2 % (16 * group_size) == 0:
        gram_matrix = sum_over_devices(packed, group_size)
    else:
        gram_matrix = unpack_whole(lax.psum(packed, "rows"))
    gram_matrix, picked = lax.optimization_barrier((gram_matrix, picked))
    returned = lax.all_to_all(
        picked.reshape(group_size, most, columns), "rows", split_axis=0, concat_axis=0, tiled=True
    )
    upper_factor, leverage = factor(gram_matrix, features)
    own_groups = (sample_rows - position * rows_dev) // span
    own_ranks = rank_in_group(own_groups)
    sketch = jnp.take(
        returned.reshape(group_size * most, columns), own_groups * most + own_ranks, axis=0
    )
    leverage = leverage.reshape(rows_dev) * (rows_dev * group_size / columns)
    return (sketch, upper_factor, leverage)


def solution(mesh):
    placed = (P("rows", None), P("rows"), P("rows"))
    return jax.shard_map(
        shards,
        mesh=mesh,
        in_specs=placed,
        out_specs=(P("rows", None), P(), P("rows")),
        check_vma=False,
    )
```

```python
import functools
import math

import jax
import jax.numpy as jnp
import numpy as np
from jax import lax
from jax.experimental import pallas as pl
from jax.experimental.pallas import tpu as pltpu
from jax.sharding import PartitionSpec as P

FACTOR = 128
SAMPLES = 4096
BLOCK = 128
PANEL = 16
F32 = jnp.float32
BF16 = jnp.bfloat16


def hadamard_array(dimension):
    table = np.ones((1, 1), np.float32)
    while table.shape[0] < dimension:
        table = np.block([[table, table], [table, -table]])
    return table


def halves(x):
    high = x.astype(BF16).astype(F32)
    return high, x - high


def dot3(a, b):
    a_high, a_low = halves(a)
    b_high, b_low = halves(b)
    left = jnp.concatenate([a_high, a_high, a_low], axis=1).astype(BF16)
    right = jnp.concatenate([b_high, b_low, b_high], axis=0).astype(BF16)
    return jnp.dot(left, right, preferred_element_type=F32)


def dot3_t(a, b):
    a_high, a_low = halves(a)
    b_high, b_low = halves(b)
    left = jnp.concatenate([a_high, a_high, a_low], axis=0).T.astype(BF16)
    right = jnp.concatenate([b_high, b_low, b_high], axis=0).astype(BF16)
    return jnp.dot(left, right, preferred_element_type=F32)


def transform_kernel(table_ref, signs_ref, features_ref, out_ref):
    groups = signs_ref.shape[0]
    table = table_ref[...]
    inner = []
    for b in range(groups):
        signed = (table * signs_ref[b : b + 1, :].astype(F32)).astype(BF16)
        rows = features_ref[b * FACTOR : (b + 1) * FACTOR, :]
        product = jnp.dot(signed, rows, preferred_element_type=F32)
        inner.append(product.astype(BF16).astype(F32))
    step = 1
    while step < groups:
        mixed = list(inner)
        for b in range(groups):
            if b & step == 0:
                mixed[b] = inner[b] + inner[b + step]
                mixed[b + step] = inner[b] - inner[b + step]
        inner = mixed
        step *= 2
    for b in range(groups):
        out_ref[b * FACTOR : (b + 1) * FACTOR, :] = inner[b].astype(BF16)


def transform(features, flip_signs):
    rows_dev, columns = features.shape
    tile = 128
    groups = rows_dev // FACTOR
    return pl.pallas_call(
        transform_kernel,
        grid=(columns // tile,),
        out_shape=jax.ShapeDtypeStruct((rows_dev, columns), BF16),
        in_specs=[
            pl.BlockSpec((FACTOR, FACTOR), lambda i: (0, 0)),
            pl.BlockSpec((groups, FACTOR), lambda i: (0, 0)),
            pl.BlockSpec((rows_dev, tile), lambda i: (0, i)),
        ],
        out_specs=pl.BlockSpec((rows_dev, tile), lambda i: (0, i)),
        compiler_params=pltpu.CompilerParams(vmem_limit_bytes=32 * 2**20),
        name="local_transform",
    )(jnp.asarray(hadamard_array(FACTOR)), flip_signs.reshape(groups, FACTOR), features)


def place_of(device):
    return {"rows": device}


def greet_all(me, size):
    barrier = pltpu.get_barrier_semaphore()

    def signal(offset, carry):
        pl.semaphore_signal(
            barrier,
            inc=1,
            device_id=place_of(lax.rem(me + offset, size)),
            device_id_type=pl.DeviceIdType.MESH,
        )
        return carry

    lax.fori_loop(1, size, signal, 0)
    pl.semaphore_wait(barrier, size - 1)


def exchange_kernel(pieces_ref, rows_ref, received_ref, wanted_ref, send, recv, row_send, row_recv):
    size = pieces_ref.shape[0]
    me = lax.axis_index("rows")
    greet_all(me, size)

    def copies(step):
        offset = 1 + lax.rem(size // 2 - 1 + step, size - 1)
        partner = lax.rem(me + offset, size)
        rows = pltpu.make_async_remote_copy(
            src_ref=rows_ref.at[0],
            dst_ref=wanted_ref.at[me],
            send_sem=row_send.at[offset],
            recv_sem=row_recv.at[offset],
            device_id=place_of(partner),
            device_id_type=pl.DeviceIdType.MESH,
        )
        data = pltpu.make_async_remote_copy(
            src_ref=pieces_ref.at[partner],
            dst_ref=received_ref.at[me],
            send_sem=send.at[offset],
            recv_sem=recv.at[offset],
            device_id=place_of(partner),
            device_id_type=pl.DeviceIdType.MESH,
        )
        return rows, data

    def begin(step, carry):
        for copy in copies(step):
            copy.start()
        return carry

    lax.fori_loop(0, size - 1, begin, 0)
    received_ref[me] = pieces_ref[me]
    wanted_ref[me] = rows_ref[0]

    def finish(step, carry):
        for copy in copies(step):
            copy.wait()
        return carry

    lax.fori_loop(0, size - 1, finish, 0)


def exchange(pieces, sample_rows):
    size = pieces.shape[0]
    samples = sample_rows.shape[0]
    vmem = pl.BlockSpec(memory_space=pltpu.VMEM)
    received, wanted = pl.pallas_call(
        exchange_kernel,
        out_shape=(
            jax.ShapeDtypeStruct(pieces.shape, pieces.dtype),
            jax.ShapeDtypeStruct((size, 1, samples), jnp.int32),
        ),
        in_specs=[vmem, vmem],
        out_specs=(vmem, vmem),
        scratch_shapes=[pltpu.SemaphoreType.DMA((size,))] * 4,
        compiler_params=pltpu.CompilerParams(
            collective_id=1, has_side_effects=True, vmem_limit_bytes=24 * 2**20
        ),
        name="exchange_rows",
    )(pieces, sample_rows.reshape(1, 1, samples))
    return received, wanted.reshape(size, samples)


def sum_kernel(
    orders, packed_ref, picked_ref, gram_ref, sketch_ref,
    work, land, summed, returned, send, recv, row_send, row_recv,
):
    me = lax.axis_index("rows")
    size, most = picked_ref.shape[:2]
    stages = len(orders[0])
    span = packed_ref.shape[0] // len(orders)
    bit = [me // 2**b % 2 for b in range(stages)]
    partner = [me + (1 - 2 * bit[b]) * 2**b for b in range(stages)]
    greet_all(me, size)

    def rows(start, size):
        return pl.ds(pl.multiple_of(start, 8), size)

    def reduce_part(part, order):
        start, size, landing = part * span, span, part * span
        kept = []
        for stage, b in enumerate(order):
            size //= 2
            source = packed_ref if stage == 0 else work
            kept_start = start + bit[b] * size
            copy = pltpu.make_async_remote_copy(
                src_ref=source.at[rows(start + (1 - bit[b]) * size, size), :],
                dst_ref=land.at[pl.ds(landing, size), :],
                send_sem=send.at[part, stage],
                recv_sem=recv.at[part, stage],
                device_id=place_of(partner[b]),
                device_id_type=pl.DeviceIdType.MESH,
            )
            copy.start()
            yield
            copy.wait()
            target = work if stage < stages - 1 else summed
            target[rows(kept_start, size), :] = (
                source[rows(kept_start, size), :] + land[pl.ds(landing, size), :]
            )
            landing += size
            start = kept_start
            kept.append((b, start, size))
        for stage, (b, start, size) in enumerate(reversed(kept)):
            block = summed.at[rows(start, size), :]
            copy = pltpu.make_async_remote_copy(
                src_ref=block,
                dst_ref=block,
                send_sem=send.at[part, stages + stage],
                recv_sem=recv.at[part, stages + stage],
                device_id=place_of(partner[b]),
                device_id_type=pl.DeviceIdType.MESH,
            )
            copy.start()
            yield
            copy.wait()

    def row_copy(step):
        offset = 1 + lax.rem(size // 2 - 1 + step, size - 1)
        owner = lax.rem(me + offset, size)
        return pltpu.make_async_remote_copy(
            src_ref=picked_ref.at[owner],
            dst_ref=returned.at[me],
            send_sem=row_send.at[offset],
            recv_sem=row_recv.at[offset],
            device_id=place_of(owner),
            device_id_type=pl.DeviceIdType.MESH,
        )

    def begin(step, carry):
        row_copy(step).start()
        return carry

    def finish(step, carry):
        row_copy(step).wait()
        return carry

    parts = [reduce_part(part, order) for part, order in enumerate(orders)]
    for part in parts:
        next(part)
    lax.fori_loop(0, size - 1, begin, 0)
    returned[me] = picked_ref[me]
    done = object()
    while parts:
        parts = [part for part in parts if next(part, done) is not done]
    unpack(summed, gram_ref)
    lax.fori_loop(0, size - 1, finish, 0)
    for group in range(size):
        sketch_ref[group * most : (group + 1) * most, :] = returned[group]


def blocks_of(columns):
    count = columns // BLOCK
    for i in range(count // 2):
        yield i, i, 0
        yield count - 1 - i, i, (count - i) * BLOCK


def unpack(packed_ref, gram_ref):
    columns = gram_ref.shape[0]
    for block, row, at in blocks_of(columns):
        width = columns - block * BLOCK
        gram_ref[block * BLOCK : (block + 1) * BLOCK, block * BLOCK :] = packed_ref[
            row * BLOCK : (row + 1) * BLOCK, at : at + width
        ]
        if block:
            gram_ref[block * BLOCK : (block + 1) * BLOCK, : block * BLOCK] = jnp.zeros(
                (BLOCK, block * BLOCK), F32
            )


def sum_over_devices(packed, picked):
    rows, width = packed.shape
    size, most = picked.shape[:2]
    columns = 2 * rows
    vmem = pl.BlockSpec(memory_space=pltpu.VMEM)
    bits = list(range(size.bit_length() - 1))
    other = list(bits)
    other[1], other[2] = bits[2], bits[1]
    return pl.pallas_call(
        functools.partial(sum_kernel, (bits, other)),
        out_shape=(
            jax.ShapeDtypeStruct((columns, columns), F32),
            jax.ShapeDtypeStruct((size * most, columns), F32),
        ),
        in_specs=[vmem, vmem],
        out_specs=(vmem, vmem),
        scratch_shapes=[
            pltpu.VMEM((rows, width), F32),
            pltpu.VMEM((rows, width), F32),
            pltpu.VMEM((rows, width), F32),
            pltpu.VMEM(picked.shape, F32),
            pltpu.SemaphoreType.DMA((2, 2 * len(bits))),
            pltpu.SemaphoreType.DMA((2, 2 * len(bits))),
            pltpu.SemaphoreType.DMA((size,)),
            pltpu.SemaphoreType.DMA((size,)),
        ],
        compiler_params=pltpu.CompilerParams(
            collective_id=2, has_side_effects=True, vmem_limit_bytes=24 * 2**20
        ),
        name="sum_grams",
    )(packed, picked)


def unpack_whole(packed):
    columns = 2 * packed.shape[0]
    gram = jnp.zeros((columns, columns), F32)
    for block, row, at in blocks_of(columns):
        width = columns - block * BLOCK
        part = packed[row * BLOCK : (row + 1) * BLOCK, at : at + width]
        gram = lax.dynamic_update_slice(gram, part, (block * BLOCK, block * BLOCK))
    return gram


def combine_kernel(most, span, rows_dev, position_ref, wanted_ref, received_ref, picked_ref, packed_ref):
    slots, samples = wanted_ref.shape
    total = received_ref.shape[0]
    position = position_ref[0]
    row_id = lax.broadcasted_iota(jnp.int32, (slots, samples), 0)
    inside = wanted_ref[...] - row_id // most * rows_dev - position * span
    mine = (inside >= 0) & (inside < span)
    earlier = (
        lax.broadcasted_iota(jnp.int32, (samples, samples), 0)
        < lax.broadcasted_iota(jnp.int32, (samples, samples), 1)
    )
    rank = jnp.dot(
        jnp.where(mine, 1.0, 0.0).astype(BF16),
        jnp.where(earlier, 1.0, 0.0).astype(BF16),
        preferred_element_type=F32,
    )
    hit = mine & (rank == (row_id % most).astype(F32))
    place = jnp.max(jnp.where(hit, inside, -1), axis=1, keepdims=True)
    to_block = lax.broadcasted_iota(jnp.int32, (slots, total), 0) // most
    column = lax.broadcasted_iota(jnp.int32, (slots, total), 1)
    bits = to_block & (column // span)
    shift = 16
    while shift >= 1:
        bits = bits ^ (bits >> shift)
        shift //= 2
    sign = (1 - 2 * (bits & 1)).astype(F32)
    choose = jnp.where(column % span == place, sign, 0.0).astype(BF16)
    picked = jnp.dot(choose, received_ref[...], preferred_element_type=F32)
    picked = picked * (1.0 / math.sqrt(SAMPLES))
    for group in range(slots // most):
        picked_ref[group] = picked[group * most : (group + 1) * most, :]
    high, low = halves(picked)
    left = jnp.concatenate([high, high, low], axis=0).T.astype(BF16)
    right = jnp.concatenate([high, low, high], axis=0).astype(BF16)
    columns = picked.shape[1]
    for block, row, at in blocks_of(columns):
        start = block * BLOCK
        packed_ref[row * BLOCK : (row + 1) * BLOCK, at : at + columns - start] = jnp.dot(
            left[start : start + BLOCK, :], right[:, start:], preferred_element_type=F32
        )


def combine(wanted, received, position, most, span, rows_dev):
    slots = wanted.shape[0] * most
    columns = received.shape[1]
    repeated = jnp.repeat(wanted, most, axis=0)
    vmem = pl.BlockSpec(memory_space=pltpu.VMEM)
    return pl.pallas_call(
        functools.partial(combine_kernel, most, span, rows_dev),
        out_shape=(
            jax.ShapeDtypeStruct((wanted.shape[0], most, columns), F32),
            jax.ShapeDtypeStruct((columns // 2, columns + BLOCK), F32),
        ),
        in_specs=[pl.BlockSpec(memory_space=pltpu.SMEM), vmem, vmem],
        out_specs=(vmem, vmem),
        compiler_params=pltpu.CompilerParams(vmem_limit_bytes=32 * 2**20),
        name="combine_pick_gram",
    )(position.reshape(1), repeated, received)


def factor_block(work_ref):
    row_id = lax.broadcasted_iota(jnp.int32, (PANEL, BLOCK), 0)
    for start in range(0, BLOCK, PANEL):
        left = work_ref[start : start + PANEL, :BLOCK]
        right = work_ref[start : start + PANEL, BLOCK:]
        cols = [
            jnp.broadcast_to(left[:, start + j : start + j + 1], (PANEL, BLOCK))
            for j in range(PANEL)
        ]
        for j in range(PANEL):
            root = lax.rsqrt(cols[j][j : j + 1, :])
            scaled = cols[j] * root
            for later in range(j + 1, PANEL):
                cols[later] = cols[later] - scaled * (cols[later][j : j + 1, :] * root)
            left_row = left[j : j + 1, :] * root
            right_row = right[j : j + 1, :] * root
            below = jnp.where(row_id > j, scaled, 0.0)
            left = jnp.where(row_id == j, left_row, left - below * left_row)
            right = jnp.where(row_id == j, right_row, right - below * right_row)
        work_ref[start : start + PANEL, :BLOCK] = left
        work_ref[start : start + PANEL, BLOCK:] = right
        rest = start + PANEL
        if rest < BLOCK:
            update = dot3_t(left, jnp.concatenate([left, right], axis=1))
            work_ref[rest:, :] = work_ref[rest:, :] - update[rest:, :]


def factor_kernel(
    scale, gram_ref, features_hbm, upper_ref, leverage_ref,
    state_ref, work_ref, right_ref, features_ref, copy_sem,
):
    columns = gram_ref.shape[0]
    count = columns // BLOCK
    fetch = pltpu.make_async_copy(features_hbm, features_ref, copy_sem)
    fetch.start()
    state_ref[...] = gram_ref[...]
    row_id = lax.broadcasted_iota(jnp.int32, (BLOCK, BLOCK), 0)
    col_id = lax.broadcasted_iota(jnp.int32, (BLOCK, BLOCK), 1)
    wide_id = lax.broadcasted_iota(jnp.int32, (BLOCK, columns), 1)

    def outer(k, carry):
        here = pl.multiple_of(k * BLOCK, BLOCK)
        rows = pl.ds(here, BLOCK)
        work_ref[:, :BLOCK] = state_ref[rows, rows]
        work_ref[:, BLOCK:] = jnp.where(row_id == col_id, 1.0, 0.0)
        factor_block(work_ref)
        inverse = jnp.where(col_id <= row_id, work_ref[:, BLOCK:], 0.0)
        panel = dot3(inverse, state_ref[rows, :])
        upper_ref[rows, :] = jnp.where(wide_id >= here + BLOCK, panel, 0.0)
        upper_ref[rows, rows] = jnp.where(col_id >= row_id, work_ref[:, :BLOCK], 0.0)
        state_ref[rows, :] = panel
        state_ref[rows, rows] = inverse
        high, low = halves(state_ref[rows, :])
        right_ref[...] = jnp.concatenate([high, low, high], axis=0).astype(BF16)

        def trailing(i, carry):
            below = pl.ds(pl.multiple_of(i * BLOCK, BLOCK), BLOCK)
            part = upper_ref[rows, below].T
            p_high, p_low = halves(part)
            left = jnp.concatenate([p_high, p_high, p_low], axis=1).astype(BF16)
            state_ref[below, rows] = jnp.zeros((BLOCK, BLOCK), F32)
            state_ref[below, :] = state_ref[below, :] - jnp.dot(
                left, right_ref[...], preferred_element_type=F32
            )
            return carry

        return lax.fori_loop(k + 1, count, trailing, carry)

    lax.fori_loop(0, count, outer, 0)
    fetch.wait()
    total = jnp.zeros((1, features_ref.shape[0]), F32)
    tile = 2 * BLOCK
    for start in range(0, columns, tile):
        depth = start + tile
        block = state_ref[start:depth, :depth]
        keep = (
            lax.broadcasted_iota(jnp.int32, (tile, depth), 1)
            <= lax.broadcasted_iota(jnp.int32, (tile, depth), 0) + start
        )
        high, low = halves(jnp.where(keep, block, 0.0))
        stacked = jnp.concatenate([high, low], axis=0).astype(BF16)
        solved = lax.dot_general(
            stacked,
            features_ref[:, :depth],
            (((1,), (1,)), ((), ())),
            preferred_element_type=F32,
        )
        solved = solved[:tile] + solved[tile:]
        total = total + jnp.sum(solved * solved, axis=0, keepdims=True)
    leverage_ref[...] = total * scale


def factor(gram, features, scale):
    columns = gram.shape[0]
    rows_dev = features.shape[0]
    vmem = pl.BlockSpec(memory_space=pltpu.VMEM)
    return pl.pallas_call(
        functools.partial(factor_kernel, scale),
        out_shape=(
            jax.ShapeDtypeStruct((columns, columns), F32),
            jax.ShapeDtypeStruct((1, rows_dev), F32),
        ),
        in_specs=[vmem, pl.BlockSpec(memory_space=pl.ANY)],
        out_specs=(vmem, vmem),
        scratch_shapes=[
            pltpu.VMEM((columns, columns), F32),
            pltpu.VMEM((BLOCK, 2 * BLOCK), F32),
            pltpu.VMEM((3 * BLOCK, columns), BF16),
            pltpu.VMEM(features.shape, BF16),
            pltpu.SemaphoreType.DMA,
        ],
        compiler_params=pltpu.CompilerParams(vmem_limit_bytes=40 * 2**20),
        cost_estimate=pl.CostEstimate(
            flops=20 * columns**3, bytes_accessed=16 * columns**2, transcendentals=0
        ),
        name="cholesky_leverage",
    )(gram, features)


def rank_in_group(group_of):
    count = group_of.shape[-1]
    same = group_of[:, None] == group_of[None, :]
    order = jnp.arange(count, dtype=jnp.int32)
    before = order[:, None] < order[None, :]
    return jnp.sum((same & before).astype(jnp.int32), axis=0)


def shards(features, flip_signs, sample_rows):
    rows_dev, columns = features.shape
    group_size = lax.axis_size("rows")
    position = lax.axis_index("rows")
    span = rows_dev // group_size
    samp_dev = sample_rows.shape[0]
    most = max(1, samp_dev // group_size)
    pieces = transform(features, flip_signs).reshape(group_size, span, columns)
    if span % 16 == 0:
        received, wanted = exchange(pieces, sample_rows)
    else:
        wanted = lax.all_gather(sample_rows, "rows", axis=0, tiled=True)
        wanted = wanted.reshape(group_size, samp_dev)
        received = lax.all_to_all(pieces, "rows", split_axis=0, concat_axis=0, tiled=True)
    picked, packed = combine(
        wanted, received.reshape(rows_dev, columns), position, most, span, rows_dev
    )
    own_scale = rows_dev * group_size / columns
    if (
        4 < group_size
        and columns // 2 % (16 * group_size) == 0
        and group_size * most == samp_dev
    ):
        gram_matrix, sketch = sum_over_devices(packed, picked)
        upper_factor, leverage = factor(gram_matrix, features, own_scale)
        return (sketch, upper_factor, leverage.reshape(rows_dev))
    gram_matrix = unpack_whole(lax.psum(packed, "rows"))
    gram_matrix, picked = lax.optimization_barrier((gram_matrix, picked))
    returned = lax.all_to_all(picked, "rows", split_axis=0, concat_axis=0, tiled=True)
    upper_factor, leverage = factor(gram_matrix, features, own_scale)
    own_groups = (sample_rows - position * rows_dev) // span
    own_ranks = rank_in_group(own_groups)
    sketch = jnp.take(
        returned.reshape(group_size * most, columns), own_groups * most + own_ranks, axis=0
    )
    return (sketch, upper_factor, leverage.reshape(rows_dev))


def solution(mesh):
    placed = (P("rows", None), P("rows"), P("rows"))
    return jax.shard_map(
        shards,
        mesh=mesh,
        in_specs=placed,
        out_specs=(P("rows", None), P(), P("rows")),
        check_vma=False,
    )
```

```python
import functools
import math

import jax
import jax.numpy as jnp
import numpy as np
from jax import lax
from jax.experimental import pallas as pl
from jax.experimental.pallas import tpu as pltpu
from jax.sharding import PartitionSpec as P

FACTOR = 128
SAMPLES = 4096
BLOCK = 128
PANEL = 16
F32 = jnp.float32
BF16 = jnp.bfloat16


def hadamard_array(dimension):
    table = np.ones((1, 1), np.float32)
    while table.shape[0] < dimension:
        table = np.block([[table, table], [table, -table]])
    return table


def halves(x):
    high = x.astype(BF16).astype(F32)
    return high, x - high


def dot3(a, b):
    a_high, a_low = halves(a)
    b_high, b_low = halves(b)
    left = jnp.concatenate([a_high, a_high, a_low], axis=1).astype(BF16)
    right = jnp.concatenate([b_high, b_low, b_high], axis=0).astype(BF16)
    return jnp.dot(left, right, preferred_element_type=F32)


def dot3_t(a, b):
    a_high, a_low = halves(a)
    b_high, b_low = halves(b)
    left = jnp.concatenate([a_high, a_high, a_low], axis=0).T.astype(BF16)
    right = jnp.concatenate([b_high, b_low, b_high], axis=0).astype(BF16)
    return jnp.dot(left, right, preferred_element_type=F32)


def transform_tile(table_ref, signs_ref, features_ref, source, out_ref, target):
    groups = signs_ref.shape[0]
    table = table_ref[...]
    inner = []
    for b in range(groups):
        signed = (table * signs_ref[b : b + 1, :].astype(F32)).astype(BF16)
        rows = features_ref[b * FACTOR : (b + 1) * FACTOR, source]
        product = jnp.dot(signed, rows, preferred_element_type=F32)
        inner.append(product.astype(BF16).astype(F32))
    step = 1
    while step < groups:
        mixed = list(inner)
        for b in range(groups):
            if b & step == 0:
                mixed[b] = inner[b] + inner[b + step]
                mixed[b + step] = inner[b] - inner[b + step]
        inner = mixed
        step *= 2
    for b in range(groups):
        out_ref[b * FACTOR : (b + 1) * FACTOR, target] = inner[b].astype(BF16)


def transform_kernel(table_ref, signs_ref, features_ref, out_ref):
    every = slice(None)
    transform_tile(table_ref, signs_ref, features_ref, every, out_ref, every)


def transform(features, flip_signs):
    rows_dev, columns = features.shape
    tile = 128
    groups = rows_dev // FACTOR
    return pl.pallas_call(
        transform_kernel,
        grid=(columns // tile,),
        out_shape=jax.ShapeDtypeStruct((rows_dev, columns), BF16),
        in_specs=[
            pl.BlockSpec((FACTOR, FACTOR), lambda i: (0, 0)),
            pl.BlockSpec((groups, FACTOR), lambda i: (0, 0)),
            pl.BlockSpec((rows_dev, tile), lambda i: (0, i)),
        ],
        out_specs=pl.BlockSpec((rows_dev, tile), lambda i: (0, i)),
        compiler_params=pltpu.CompilerParams(vmem_limit_bytes=32 * 2**20),
        name="local_transform",
    )(jnp.asarray(hadamard_array(FACTOR)), flip_signs.reshape(groups, FACTOR), features)


def place_of(device):
    return {"rows": device}


def greet_all(me, size):
    barrier = pltpu.get_barrier_semaphore()

    def signal(offset, carry):
        pl.semaphore_signal(
            barrier,
            inc=1,
            device_id=place_of(lax.rem(me + offset, size)),
            device_id_type=pl.DeviceIdType.MESH,
        )
        return carry

    lax.fori_loop(1, size, signal, 0)


def await_all(size):
    pl.semaphore_wait(pltpu.get_barrier_semaphore(), size - 1)


def exchange_kernel(
    table_ref, signs_ref, features_ref, rows_ref, received_ref, wanted_ref,
    pieces, send, recv, row_send, row_recv,
):
    size = wanted_ref.shape[0]
    parts, rows_dev, part_columns = received_ref.shape
    span = rows_dev // size
    me = lax.axis_index("rows")
    greet_all(me, size)

    def slab(device):
        return pl.ds(pl.multiple_of(device * span, 16), span)

    def place(step):
        offset = 1 + lax.rem(size // 2 - 1 + step, size - 1)
        return offset, lax.rem(me + offset, size)

    def row_copy(step):
        offset, partner = place(step)
        return pltpu.make_async_remote_copy(
            src_ref=rows_ref.at[0],
            dst_ref=wanted_ref.at[me],
            send_sem=row_send.at[offset],
            recv_sem=row_recv.at[offset],
            device_id=place_of(partner),
            device_id_type=pl.DeviceIdType.MESH,
        )

    def data_copy(part, step):
        offset, partner = place(step)
        return pltpu.make_async_remote_copy(
            src_ref=pieces.at[part, slab(partner), :],
            dst_ref=received_ref.at[part, slab(me), :],
            send_sem=send.at[part, offset],
            recv_sem=recv.at[part, offset],
            device_id=place_of(partner),
            device_id_type=pl.DeviceIdType.MESH,
        )

    def begin_rows(step, carry):
        row_copy(step).start()
        return carry

    for part in range(parts):

        def tile(i, carry):
            source = pl.ds(pl.multiple_of(part * part_columns + i * FACTOR, FACTOR), FACTOR)
            target = pl.ds(pl.multiple_of(i * FACTOR, FACTOR), FACTOR)
            transform_tile(
                table_ref, signs_ref, features_ref, source, pieces.at[part], target
            )
            return carry

        lax.fori_loop(0, part_columns // FACTOR, tile, 0)
        if part == 0:
            await_all(size)

        def begin(step, carry):
            data_copy(part, step).start()
            return carry

        lax.fori_loop(0, size - 1, begin, 0)
    lax.fori_loop(0, size - 1, begin_rows, 0)
    for part in range(parts):
        received_ref[part, slab(me), :] = pieces[part, slab(me), :]
    wanted_ref[me] = rows_ref[0]

    def finish(step, carry):
        for part in range(parts):
            data_copy(part, step).wait()
        row_copy(step).wait()
        return carry

    lax.fori_loop(0, size - 1, finish, 0)


def exchange(features, flip_signs, sample_rows, size):
    rows_dev, columns = features.shape
    groups = rows_dev // FACTOR
    samples = sample_rows.shape[0]
    parts = 2
    shape = (parts, rows_dev, columns // parts)
    vmem = pl.BlockSpec(memory_space=pltpu.VMEM)
    received, wanted = pl.pallas_call(
        exchange_kernel,
        out_shape=(
            jax.ShapeDtypeStruct(shape, BF16),
            jax.ShapeDtypeStruct((size, 1, samples), jnp.int32),
        ),
        in_specs=[vmem] * 4,
        out_specs=(vmem, vmem),
        scratch_shapes=[
            pltpu.VMEM(shape, BF16),
            pltpu.SemaphoreType.DMA((parts, size)),
            pltpu.SemaphoreType.DMA((parts, size)),
            pltpu.SemaphoreType.DMA((size,)),
            pltpu.SemaphoreType.DMA((size,)),
        ],
        compiler_params=pltpu.CompilerParams(
            collective_id=1, has_side_effects=True, vmem_limit_bytes=24 * 2**20
        ),
        name="transform_exchange",
    )(
        jnp.asarray(hadamard_array(FACTOR)),
        flip_signs.reshape(groups, FACTOR),
        features,
        sample_rows.reshape(1, 1, samples),
    )
    return received, wanted.reshape(size, samples)


def sum_kernel(orders, packed_ref, gram_ref, work, land, summed, send, recv):
    me = lax.axis_index("rows")
    stages = len(orders[0])
    span = packed_ref.shape[0] // len(orders)
    bit = [me // 2**b % 2 for b in range(stages)]
    partner = [me + (1 - 2 * bit[b]) * 2**b for b in range(stages)]
    greet_all(me, 2**stages)
    await_all(2**stages)

    def rows(start, size):
        return pl.ds(pl.multiple_of(start, 8), size)

    def reduce_part(part, order):
        start, size, landing = part * span, span, part * span
        kept = []
        for stage, b in enumerate(order):
            size //= 2
            source = packed_ref if stage == 0 else work
            kept_start = start + bit[b] * size
            copy = pltpu.make_async_remote_copy(
                src_ref=source.at[rows(start + (1 - bit[b]) * size, size), :],
                dst_ref=land.at[pl.ds(landing, size), :],
                send_sem=send.at[part, stage],
                recv_sem=recv.at[part, stage],
                device_id=place_of(partner[b]),
                device_id_type=pl.DeviceIdType.MESH,
            )
            copy.start()
            yield
            copy.wait()
            target = work if stage < stages - 1 else summed
            target[rows(kept_start, size), :] = (
                source[rows(kept_start, size), :] + land[pl.ds(landing, size), :]
            )
            landing += size
            start = kept_start
            kept.append((b, start, size))
        for stage, (b, start, size) in enumerate(reversed(kept)):
            block = summed.at[rows(start, size), :]
            copy = pltpu.make_async_remote_copy(
                src_ref=block,
                dst_ref=block,
                send_sem=send.at[part, stages + stage],
                recv_sem=recv.at[part, stages + stage],
                device_id=place_of(partner[b]),
                device_id_type=pl.DeviceIdType.MESH,
            )
            copy.start()
            yield
            copy.wait()

    parts = [reduce_part(part, order) for part, order in enumerate(orders)]
    done = object()
    while parts:
        parts = [part for part in parts if next(part, done) is not done]
    unpack(summed, gram_ref)


def blocks_of(columns):
    count = columns // BLOCK
    for i in range(count // 2):
        yield i, i, 0
        yield count - 1 - i, i, (count - i) * BLOCK


def unpack(packed_ref, gram_ref):
    columns = gram_ref.shape[0]
    for block, row, at in blocks_of(columns):
        width = columns - block * BLOCK
        gram_ref[block * BLOCK : (block + 1) * BLOCK, block * BLOCK :] = packed_ref[
            row * BLOCK : (row + 1) * BLOCK, at : at + width
        ]
        if block:
            gram_ref[block * BLOCK : (block + 1) * BLOCK, : block * BLOCK] = jnp.zeros(
                (BLOCK, block * BLOCK), F32
            )


def sum_over_devices(packed, size):
    rows, width = packed.shape
    columns = 2 * rows
    vmem = pl.BlockSpec(memory_space=pltpu.VMEM)
    bits = list(range(size.bit_length() - 1))
    other = list(bits)
    other[1], other[2] = bits[2], bits[1]
    return pl.pallas_call(
        functools.partial(sum_kernel, (bits, other)),
        out_shape=jax.ShapeDtypeStruct((columns, columns), F32),
        in_specs=[vmem],
        out_specs=vmem,
        scratch_shapes=[
            pltpu.VMEM((rows, width), F32),
            pltpu.VMEM((rows, width), F32),
            pltpu.VMEM((rows, width), F32),
            pltpu.SemaphoreType.DMA((2, 2 * len(bits))),
            pltpu.SemaphoreType.DMA((2, 2 * len(bits))),
        ],
        compiler_params=pltpu.CompilerParams(
            collective_id=2, has_side_effects=True, vmem_limit_bytes=24 * 2**20
        ),
        name="sum_grams",
    )(packed)


def unpack_whole(packed):
    columns = 2 * packed.shape[0]
    gram = jnp.zeros((columns, columns), F32)
    for block, row, at in blocks_of(columns):
        width = columns - block * BLOCK
        part = packed[row * BLOCK : (row + 1) * BLOCK, at : at + width]
        gram = lax.dynamic_update_slice(gram, part, (block * BLOCK, block * BLOCK))
    return gram


def combine_kernel(most, span, rows_dev, position_ref, wanted_ref, received_ref, picked_ref, packed_ref):
    slots, samples = wanted_ref.shape
    total = received_ref.shape[1]
    position = position_ref[0]
    row_id = lax.broadcasted_iota(jnp.int32, (slots, samples), 0)
    inside = wanted_ref[...] - row_id // most * rows_dev - position * span
    mine = (inside >= 0) & (inside < span)
    earlier = (
        lax.broadcasted_iota(jnp.int32, (samples, samples), 0)
        < lax.broadcasted_iota(jnp.int32, (samples, samples), 1)
    )
    rank = jnp.dot(
        jnp.where(mine, 1.0, 0.0).astype(BF16),
        jnp.where(earlier, 1.0, 0.0).astype(BF16),
        preferred_element_type=F32,
    )
    hit = mine & (rank == (row_id % most).astype(F32))
    place = jnp.max(jnp.where(hit, inside, -1), axis=1, keepdims=True)
    to_block = lax.broadcasted_iota(jnp.int32, (slots, total), 0) // most
    column = lax.broadcasted_iota(jnp.int32, (slots, total), 1)
    bits = to_block & (column // span)
    shift = 16
    while shift >= 1:
        bits = bits ^ (bits >> shift)
        shift //= 2
    sign = (1 - 2 * (bits & 1)).astype(F32)
    choose = jnp.where(column % span == place, sign, 0.0).astype(BF16)
    picked = jnp.concatenate(
        [
            jnp.dot(choose, received_ref[part], preferred_element_type=F32)
            for part in range(received_ref.shape[0])
        ],
        axis=1,
    )
    picked = picked * (1.0 / math.sqrt(SAMPLES))
    for group in range(slots // most):
        picked_ref[group] = picked[group * most : (group + 1) * most, :]
    high, low = halves(picked)
    left = jnp.concatenate([high, high, low], axis=0).T.astype(BF16)
    right = jnp.concatenate([high, low, high], axis=0).astype(BF16)
    columns = picked.shape[1]
    for block, row, at in blocks_of(columns):
        start = block * BLOCK
        packed_ref[row * BLOCK : (row + 1) * BLOCK, at : at + columns - start] = jnp.dot(
            left[start : start + BLOCK, :], right[:, start:], preferred_element_type=F32
        )


def combine(wanted, received, position, most, span, rows_dev):
    slots = wanted.shape[0] * most
    columns = received.shape[0] * received.shape[2]
    repeated = jnp.repeat(wanted, most, axis=0)
    vmem = pl.BlockSpec(memory_space=pltpu.VMEM)
    return pl.pallas_call(
        functools.partial(combine_kernel, most, span, rows_dev),
        out_shape=(
            jax.ShapeDtypeStruct((wanted.shape[0], most, columns), F32),
            jax.ShapeDtypeStruct((columns // 2, columns + BLOCK), F32),
        ),
        in_specs=[pl.BlockSpec(memory_space=pltpu.SMEM), vmem, vmem],
        out_specs=(vmem, vmem),
        compiler_params=pltpu.CompilerParams(vmem_limit_bytes=32 * 2**20),
        name="combine_pick_gram",
    )(position.reshape(1), repeated, received)


def factor_block(work_ref):
    row_id = lax.broadcasted_iota(jnp.int32, (PANEL, BLOCK), 0)
    for start in range(0, BLOCK, PANEL):
        left = work_ref[start : start + PANEL, :BLOCK]
        right = work_ref[start : start + PANEL, BLOCK:]
        cols = [
            jnp.broadcast_to(left[:, start + j : start + j + 1], (PANEL, BLOCK))
            for j in range(PANEL)
        ]
        for j in range(PANEL):
            root = lax.rsqrt(cols[j][j : j + 1, :])
            scaled = cols[j] * root
            for later in range(j + 1, PANEL):
                cols[later] = cols[later] - scaled * (cols[later][j : j + 1, :] * root)
            left_row = left[j : j + 1, :] * root
            right_row = right[j : j + 1, :] * root
            below = jnp.where(row_id > j, scaled, 0.0)
            left = jnp.where(row_id == j, left_row, left - below * left_row)
            right = jnp.where(row_id == j, right_row, right - below * right_row)
        work_ref[start : start + PANEL, :BLOCK] = left
        work_ref[start : start + PANEL, BLOCK:] = right
        rest = start + PANEL
        if rest < BLOCK:
            update = dot3_t(left, jnp.concatenate([left, right], axis=1))
            work_ref[rest:, :] = work_ref[rest:, :] - update[rest:, :]


def factor_kernel(
    scale, gram_ref, features_hbm, upper_ref, leverage_ref,
    state_ref, work_ref, right_ref, features_ref, copy_sem,
):
    columns = gram_ref.shape[0]
    count = columns // BLOCK
    fetch = pltpu.make_async_copy(features_hbm, features_ref, copy_sem)
    fetch.start()
    state_ref[...] = gram_ref[...]
    row_id = lax.broadcasted_iota(jnp.int32, (BLOCK, BLOCK), 0)
    col_id = lax.broadcasted_iota(jnp.int32, (BLOCK, BLOCK), 1)
    wide_id = lax.broadcasted_iota(jnp.int32, (BLOCK, columns), 1)

    def outer(k, carry):
        here = pl.multiple_of(k * BLOCK, BLOCK)
        rows = pl.ds(here, BLOCK)
        work_ref[:, :BLOCK] = state_ref[rows, rows]
        work_ref[:, BLOCK:] = jnp.where(row_id == col_id, 1.0, 0.0)
        factor_block(work_ref)
        inverse = jnp.where(col_id <= row_id, work_ref[:, BLOCK:], 0.0)
        panel = dot3(inverse, state_ref[rows, :])
        upper_ref[rows, :] = jnp.where(wide_id >= here + BLOCK, panel, 0.0)
        upper_ref[rows, rows] = jnp.where(col_id >= row_id, work_ref[:, :BLOCK], 0.0)
        state_ref[rows, :] = panel
        state_ref[rows, rows] = inverse
        high, low = halves(state_ref[rows, :])
        right_ref[...] = jnp.concatenate([high, low, high], axis=0).astype(BF16)

        def trailing(i, carry):
            below = pl.ds(pl.multiple_of(i * BLOCK, BLOCK), BLOCK)
            part = upper_ref[rows, below].T
            p_high, p_low = halves(part)
            left = jnp.concatenate([p_high, p_high, p_low], axis=1).astype(BF16)
            state_ref[below, rows] = jnp.zeros((BLOCK, BLOCK), F32)
            state_ref[below, :] = state_ref[below, :] - jnp.dot(
                left, right_ref[...], preferred_element_type=F32
            )
            return carry

        return lax.fori_loop(k + 1, count, trailing, carry)

    lax.fori_loop(0, count, outer, 0)
    fetch.wait()
    total = jnp.zeros((1, features_ref.shape[0]), F32)
    tile = 2 * BLOCK
    for start in range(0, columns, tile):
        depth = start + tile
        block = state_ref[start:depth, :depth]
        keep = (
            lax.broadcasted_iota(jnp.int32, (tile, depth), 1)
            <= lax.broadcasted_iota(jnp.int32, (tile, depth), 0) + start
        )
        high, low = halves(jnp.where(keep, block, 0.0))
        stacked = jnp.concatenate([high, low], axis=0).astype(BF16)
        solved = lax.dot_general(
            stacked,
            features_ref[:, :depth],
            (((1,), (1,)), ((), ())),
            preferred_element_type=F32,
        )
        solved = solved[:tile] + solved[tile:]
        total = total + jnp.sum(solved * solved, axis=0, keepdims=True)
    leverage_ref[...] = total * scale


def factor_return_kernel(
    scale, gram_ref, features_hbm, picked_ref, upper_ref, leverage_ref, sketch_ref,
    state_ref, work_ref, right_ref, features_ref, copy_sem, returned, row_send, row_recv,
):
    me = lax.axis_index("rows")
    size, most = picked_ref.shape[:2]
    greet_all(me, size)
    await_all(size)

    def row_copy(step):
        offset = 1 + lax.rem(size // 2 - 1 + step, size - 1)
        owner = lax.rem(me + offset, size)
        return pltpu.make_async_remote_copy(
            src_ref=picked_ref.at[owner],
            dst_ref=returned.at[me],
            send_sem=row_send.at[offset],
            recv_sem=row_recv.at[offset],
            device_id=place_of(owner),
            device_id_type=pl.DeviceIdType.MESH,
        )

    def begin(step, carry):
        row_copy(step).start()
        return carry

    def finish(step, carry):
        row_copy(step).wait()
        return carry

    lax.fori_loop(0, size - 1, begin, 0)
    returned[me] = picked_ref[me]
    factor_kernel(
        scale, gram_ref, features_hbm, upper_ref, leverage_ref,
        state_ref, work_ref, right_ref, features_ref, copy_sem,
    )
    lax.fori_loop(0, size - 1, finish, 0)
    for group in range(size):
        sketch_ref[group * most : (group + 1) * most, :] = returned[group]


def factor(gram, features, scale, picked=None):
    columns = gram.shape[0]
    rows_dev = features.shape[0]
    vmem = pl.BlockSpec(memory_space=pltpu.VMEM)
    kernel, inputs, more, own = factor_kernel, (gram, features), [], {}
    outputs = [
        jax.ShapeDtypeStruct((columns, columns), F32),
        jax.ShapeDtypeStruct((1, rows_dev), F32),
    ]
    if picked is not None:
        size, most = picked.shape[:2]
        kernel, inputs = factor_return_kernel, (gram, features, picked)
        outputs.append(jax.ShapeDtypeStruct((size * most, columns), F32))
        more = [
            pltpu.VMEM(picked.shape, F32),
            pltpu.SemaphoreType.DMA((size,)),
            pltpu.SemaphoreType.DMA((size,)),
        ]
        own = {"collective_id": 3, "has_side_effects": True}
    return pl.pallas_call(
        functools.partial(kernel, scale),
        out_shape=outputs,
        in_specs=[vmem, pl.BlockSpec(memory_space=pl.ANY), vmem][: len(inputs)],
        out_specs=[vmem] * len(outputs),
        scratch_shapes=[
            pltpu.VMEM((columns, columns), F32),
            pltpu.VMEM((BLOCK, 2 * BLOCK), F32),
            pltpu.VMEM((3 * BLOCK, columns), BF16),
            pltpu.VMEM(features.shape, BF16),
            pltpu.SemaphoreType.DMA,
        ]
        + more,
        compiler_params=pltpu.CompilerParams(vmem_limit_bytes=40 * 2**20, **own),
        cost_estimate=pl.CostEstimate(
            flops=20 * columns**3, bytes_accessed=16 * columns**2, transcendentals=0
        ),
        name="cholesky_leverage",
    )(*inputs)


def rank_in_group(group_of):
    count = group_of.shape[-1]
    same = group_of[:, None] == group_of[None, :]
    order = jnp.arange(count, dtype=jnp.int32)
    before = order[:, None] < order[None, :]
    return jnp.sum((same & before).astype(jnp.int32), axis=0)


def shards(features, flip_signs, sample_rows):
    rows_dev, columns = features.shape
    group_size = lax.axis_size("rows")
    position = lax.axis_index("rows")
    span = rows_dev // group_size
    samp_dev = sample_rows.shape[0]
    most = max(1, samp_dev // group_size)
    if span % 16 == 0:
        received, wanted = exchange(features, flip_signs, sample_rows, group_size)
    else:
        pieces = transform(features, flip_signs).reshape(group_size, span, columns)
        wanted = lax.all_gather(sample_rows, "rows", axis=0, tiled=True)
        wanted = wanted.reshape(group_size, samp_dev)
        received = lax.all_to_all(pieces, "rows", split_axis=0, concat_axis=0, tiled=True)
        received = received.reshape(1, rows_dev, columns)
    picked, packed = combine(wanted, received, position, most, span, rows_dev)
    own_scale = rows_dev * group_size / columns
    if (
        4 < group_size
        and columns // 2 % (16 * group_size) == 0
        and group_size * most == samp_dev
    ):
        gram_matrix = sum_over_devices(packed, group_size)
        upper_factor, leverage, sketch = factor(gram_matrix, features, own_scale, picked)
        return (sketch, upper_factor, leverage.reshape(rows_dev))
    gram_matrix = unpack_whole(lax.psum(packed, "rows"))
    gram_matrix, picked = lax.optimization_barrier((gram_matrix, picked))
    returned = lax.all_to_all(picked, "rows", split_axis=0, concat_axis=0, tiled=True)
    upper_factor, leverage = factor(gram_matrix, features, own_scale)
    own_groups = (sample_rows - position * rows_dev) // span
    own_ranks = rank_in_group(own_groups)
    sketch = jnp.take(
        returned.reshape(group_size * most, columns), own_groups * most + own_ranks, axis=0
    )
    return (sketch, upper_factor, leverage.reshape(rows_dev))


def solution(mesh):
    placed = (P("rows", None), P("rows"), P("rows"))
    return jax.shard_map(
        shards,
        mesh=mesh,
        in_specs=placed,
        out_specs=(P("rows", None), P(), P("rows")),
        check_vma=False,
    )
```

```python
import functools
import math

import jax
import jax.numpy as jnp
from jax import lax
from jax.experimental import pallas as pl
from jax.experimental.pallas import tpu as pltpu
from jax.sharding import PartitionSpec as P

FACTOR = 128
SAMPLES = 4096
BLOCK = 128
PANEL = 16
F32 = jnp.float32
BF16 = jnp.bfloat16


def hadamard_signs(rows, columns):
    bits = rows & columns
    shift = 16
    while shift >= 1:
        bits = bits ^ (bits >> shift)
        shift //= 2
    return (1 - 2 * (bits & 1)).astype(F32)


def halves(x):
    high = x.astype(BF16).astype(F32)
    return high, x - high


def dot3(a, b):
    a_high, a_low = halves(a)
    b_high, b_low = halves(b)
    left = jnp.concatenate([a_high, a_high, a_low], axis=1).astype(BF16)
    right = jnp.concatenate([b_high, b_low, b_high], axis=0).astype(BF16)
    return jnp.dot(left, right, preferred_element_type=F32)


def dot3_t(a, b):
    a_high, a_low = halves(a)
    b_high, b_low = halves(b)
    left = jnp.concatenate([a_high, a_high, a_low], axis=0).T.astype(BF16)
    right = jnp.concatenate([b_high, b_low, b_high], axis=0).astype(BF16)
    return jnp.dot(left, right, preferred_element_type=F32)


def transform_tile(signs_ref, features_ref, source, out_ref, target):
    groups = signs_ref.shape[0]
    table = hadamard_signs(
        lax.broadcasted_iota(jnp.int32, (FACTOR, FACTOR), 0),
        lax.broadcasted_iota(jnp.int32, (FACTOR, FACTOR), 1),
    )
    inner = []
    for b in range(groups):
        signed = (table * signs_ref[b : b + 1, :].astype(F32)).astype(BF16)
        rows = features_ref[b * FACTOR : (b + 1) * FACTOR, source]
        product = jnp.dot(signed, rows, preferred_element_type=F32)
        inner.append(product.astype(BF16).astype(F32))
    step = 1
    while step < groups:
        mixed = list(inner)
        for b in range(groups):
            if b & step == 0:
                mixed[b] = inner[b] + inner[b + step]
                mixed[b + step] = inner[b] - inner[b + step]
        inner = mixed
        step *= 2
    for b in range(groups):
        out_ref[b * FACTOR : (b + 1) * FACTOR, target] = inner[b].astype(BF16)


def transform_kernel(signs_ref, features_ref, out_ref):
    every = slice(None)
    transform_tile(signs_ref, features_ref, every, out_ref, every)


def transform(features, flip_signs):
    rows_dev, columns = features.shape
    tile = 128
    groups = rows_dev // FACTOR
    return pl.pallas_call(
        transform_kernel,
        grid=(columns // tile,),
        out_shape=jax.ShapeDtypeStruct((rows_dev, columns), BF16),
        in_specs=[
            pl.BlockSpec((groups, FACTOR), lambda i: (0, 0)),
            pl.BlockSpec((rows_dev, tile), lambda i: (0, i)),
        ],
        out_specs=pl.BlockSpec((rows_dev, tile), lambda i: (0, i)),
        compiler_params=pltpu.CompilerParams(vmem_limit_bytes=32 * 2**20),
        name="local_transform",
    )(flip_signs.reshape(groups, FACTOR), features)


def place_of(device):
    return {"rows": device}


def greet_all(me, size):
    barrier = pltpu.get_barrier_semaphore()

    def signal(offset, carry):
        pl.semaphore_signal(
            barrier,
            inc=1,
            device_id=place_of(lax.rem(me + offset, size)),
            device_id_type=pl.DeviceIdType.MESH,
        )
        return carry

    lax.fori_loop(1, size, signal, 0)


def await_all(size):
    pl.semaphore_wait(pltpu.get_barrier_semaphore(), size - 1)


def greet(partners):
    barrier = pltpu.get_barrier_semaphore()
    for partner in partners:
        pl.semaphore_signal(
            barrier, inc=1, device_id=place_of(partner), device_id_type=pl.DeviceIdType.MESH
        )
    pl.semaphore_wait(barrier, len(partners))


def exchange_kernel(
    signs_ref, features_ref, rows_ref, received_ref, wanted_ref,
    pieces, send, recv, row_send, row_recv,
):
    size = wanted_ref.shape[0]
    parts, rows_dev, part_columns = received_ref.shape
    span = rows_dev // size
    me = lax.axis_index("rows")
    greet_all(me, size)

    def slab(device):
        return pl.ds(pl.multiple_of(device * span, 16), span)

    def place(step):
        offset = 1 + lax.rem(size // 2 - 1 + step, size - 1)
        return offset, lax.rem(me + offset, size)

    def row_copy(step):
        offset, partner = place(step)
        return pltpu.make_async_remote_copy(
            src_ref=rows_ref.at[0],
            dst_ref=wanted_ref.at[me],
            send_sem=row_send.at[offset],
            recv_sem=row_recv.at[offset],
            device_id=place_of(partner),
            device_id_type=pl.DeviceIdType.MESH,
        )

    def data_copy(part, step):
        offset, partner = place(step)
        return pltpu.make_async_remote_copy(
            src_ref=pieces.at[part, slab(partner), :],
            dst_ref=received_ref.at[part, slab(me), :],
            send_sem=send.at[part, offset],
            recv_sem=recv.at[part, offset],
            device_id=place_of(partner),
            device_id_type=pl.DeviceIdType.MESH,
        )

    def begin_rows(step, carry):
        row_copy(step).start()
        return carry

    for part in range(parts):

        def tile(i, carry):
            source = pl.ds(pl.multiple_of(part * part_columns + i * FACTOR, FACTOR), FACTOR)
            target = pl.ds(pl.multiple_of(i * FACTOR, FACTOR), FACTOR)
            transform_tile(signs_ref, features_ref, source, pieces.at[part], target)
            return carry

        lax.fori_loop(0, part_columns // FACTOR, tile, 0)
        if part == 0:
            await_all(size)

        def begin(step, carry):
            data_copy(part, step).start()
            return carry

        lax.fori_loop(0, size - 1, begin, 0)
    lax.fori_loop(0, size - 1, begin_rows, 0)
    for part in range(parts):
        received_ref[part, slab(me), :] = pieces[part, slab(me), :]
    wanted_ref[me] = rows_ref[0]

    def finish(step, carry):
        for part in range(parts):
            data_copy(part, step).wait()
        row_copy(step).wait()
        return carry

    lax.fori_loop(0, size - 1, finish, 0)


def exchange(features, flip_signs, sample_rows, size):
    rows_dev, columns = features.shape
    groups = rows_dev // FACTOR
    samples = sample_rows.shape[0]
    parts = 2
    shape = (parts, rows_dev, columns // parts)
    vmem = pl.BlockSpec(memory_space=pltpu.VMEM)
    received, wanted = pl.pallas_call(
        exchange_kernel,
        out_shape=(
            jax.ShapeDtypeStruct(shape, BF16),
            jax.ShapeDtypeStruct((size, 1, samples), jnp.int32),
        ),
        in_specs=[vmem] * 3,
        out_specs=(vmem, vmem),
        scratch_shapes=[
            pltpu.VMEM(shape, BF16),
            pltpu.SemaphoreType.DMA((parts, size)),
            pltpu.SemaphoreType.DMA((parts, size)),
            pltpu.SemaphoreType.DMA((size,)),
            pltpu.SemaphoreType.DMA((size,)),
        ],
        compiler_params=pltpu.CompilerParams(
            collective_id=1, has_side_effects=True, vmem_limit_bytes=24 * 2**20
        ),
        name="transform_exchange",
    )(
        flip_signs.reshape(groups, FACTOR),
        features,
        sample_rows.reshape(1, 1, samples),
    )
    return received, wanted.reshape(size, samples)


def sum_kernel(orders, packed_ref, gram_ref, work, land, summed, send, recv):
    me = lax.axis_index("rows")
    stages = len(orders[0])
    span = packed_ref.shape[0] // len(orders)
    bit = [me // 2**b % 2 for b in range(stages)]
    partner = [me + (1 - 2 * bit[b]) * 2**b for b in range(stages)]
    greet(partner)

    def rows(start, size):
        return pl.ds(pl.multiple_of(start, 8), size)

    def reduce_part(part, order):
        start, size, landing = part * span, span, part * span
        kept = []
        for stage, b in enumerate(order):
            size //= 2
            source = packed_ref if stage == 0 else work
            kept_start = start + bit[b] * size
            copy = pltpu.make_async_remote_copy(
                src_ref=source.at[rows(start + (1 - bit[b]) * size, size), :],
                dst_ref=land.at[pl.ds(landing, size), :],
                send_sem=send.at[part, stage],
                recv_sem=recv.at[part, stage],
                device_id=place_of(partner[b]),
                device_id_type=pl.DeviceIdType.MESH,
            )
            copy.start()
            yield
            copy.wait()
            target = work if stage < stages - 1 else summed
            target[rows(kept_start, size), :] = (
                source[rows(kept_start, size), :] + land[pl.ds(landing, size), :]
            )
            landing += size
            start = kept_start
            kept.append((b, start, size))
        for stage, (b, start, size) in enumerate(reversed(kept)):
            block = summed.at[rows(start, size), :]
            copy = pltpu.make_async_remote_copy(
                src_ref=block,
                dst_ref=block,
                send_sem=send.at[part, stages + stage],
                recv_sem=recv.at[part, stages + stage],
                device_id=place_of(partner[b]),
                device_id_type=pl.DeviceIdType.MESH,
            )
            copy.start()
            yield
            copy.wait()

    parts = [reduce_part(part, order) for part, order in enumerate(orders)]
    done = object()
    while parts:
        parts = [part for part in parts if next(part, done) is not done]
    unpack(summed, gram_ref)


def blocks_of(columns):
    count = columns // BLOCK
    for i in range(count // 2):
        yield i, i, 0
        yield count - 1 - i, i, (count - i) * BLOCK


def unpack(packed_ref, gram_ref):
    columns = gram_ref.shape[0]
    for block, row, at in blocks_of(columns):
        width = columns - block * BLOCK
        gram_ref[block * BLOCK : (block + 1) * BLOCK, block * BLOCK :] = packed_ref[
            row * BLOCK : (row + 1) * BLOCK, at : at + width
        ]
        if block:
            gram_ref[block * BLOCK : (block + 1) * BLOCK, : block * BLOCK] = jnp.zeros(
                (BLOCK, block * BLOCK), F32
            )


def sum_over_devices(packed, size):
    rows, width = packed.shape
    columns = 2 * rows
    vmem = pl.BlockSpec(memory_space=pltpu.VMEM)
    bits = list(range(size.bit_length() - 1))
    other = list(bits)
    other[1], other[2] = bits[2], bits[1]
    return pl.pallas_call(
        functools.partial(sum_kernel, (bits, other)),
        out_shape=jax.ShapeDtypeStruct((columns, columns), F32),
        in_specs=[vmem],
        out_specs=vmem,
        scratch_shapes=[
            pltpu.VMEM((rows, width), F32),
            pltpu.VMEM((rows, width), F32),
            pltpu.VMEM((rows, width), F32),
            pltpu.SemaphoreType.DMA((2, 2 * len(bits))),
            pltpu.SemaphoreType.DMA((2, 2 * len(bits))),
        ],
        compiler_params=pltpu.CompilerParams(
            collective_id=2, has_side_effects=True, vmem_limit_bytes=24 * 2**20
        ),
        name="sum_grams",
    )(packed)


def unpack_whole(packed):
    columns = 2 * packed.shape[0]
    gram = jnp.zeros((columns, columns), F32)
    for block, row, at in blocks_of(columns):
        width = columns - block * BLOCK
        part = packed[row * BLOCK : (row + 1) * BLOCK, at : at + width]
        gram = lax.dynamic_update_slice(gram, part, (block * BLOCK, block * BLOCK))
    return gram


def combine_kernel(most, span, rows_dev, position_ref, wanted_ref, received_ref, picked_ref, packed_ref):
    slots, samples = wanted_ref.shape
    total = received_ref.shape[1]
    position = position_ref[0]
    row_id = lax.broadcasted_iota(jnp.int32, (slots, samples), 0)
    inside = wanted_ref[...] - row_id // most * rows_dev - position * span
    mine = (inside >= 0) & (inside < span)
    earlier = (
        lax.broadcasted_iota(jnp.int32, (samples, samples), 0)
        < lax.broadcasted_iota(jnp.int32, (samples, samples), 1)
    )
    rank = jnp.dot(
        jnp.where(mine, 1.0, 0.0).astype(BF16),
        jnp.where(earlier, 1.0, 0.0).astype(BF16),
        preferred_element_type=F32,
    )
    hit = mine & (rank == (row_id % most).astype(F32))
    place = jnp.max(jnp.where(hit, inside, -1), axis=1, keepdims=True)
    to_block = lax.broadcasted_iota(jnp.int32, (slots, total), 0) // most
    column = lax.broadcasted_iota(jnp.int32, (slots, total), 1)
    sign = hadamard_signs(to_block, column // span)
    choose = jnp.where(column % span == place, sign, 0.0).astype(BF16)
    picked = jnp.concatenate(
        [
            jnp.dot(choose, received_ref[part], preferred_element_type=F32)
            for part in range(received_ref.shape[0])
        ],
        axis=1,
    )
    picked = picked * (1.0 / math.sqrt(SAMPLES))
    for group in range(slots // most):
        picked_ref[group] = picked[group * most : (group + 1) * most, :]
    high, low = halves(picked)
    left = jnp.concatenate([high, high, low], axis=0).T.astype(BF16)
    right = jnp.concatenate([high, low, high], axis=0).astype(BF16)
    columns = picked.shape[1]
    for block, row, at in blocks_of(columns):
        start = block * BLOCK
        packed_ref[row * BLOCK : (row + 1) * BLOCK, at : at + columns - start] = jnp.dot(
            left[start : start + BLOCK, :], right[:, start:], preferred_element_type=F32
        )


def combine(wanted, received, position, most, span, rows_dev):
    slots = wanted.shape[0] * most
    columns = received.shape[0] * received.shape[2]
    repeated = jnp.repeat(wanted, most, axis=0)
    vmem = pl.BlockSpec(memory_space=pltpu.VMEM)
    return pl.pallas_call(
        functools.partial(combine_kernel, most, span, rows_dev),
        out_shape=(
            jax.ShapeDtypeStruct((wanted.shape[0], most, columns), F32),
            jax.ShapeDtypeStruct((columns // 2, columns + BLOCK), F32),
        ),
        in_specs=[pl.BlockSpec(memory_space=pltpu.SMEM), vmem, vmem],
        out_specs=(vmem, vmem),
        compiler_params=pltpu.CompilerParams(vmem_limit_bytes=32 * 2**20),
        name="combine_pick_gram",
    )(position.reshape(1), repeated, received)


def factor_block(work_ref):
    for start in range(0, BLOCK, PANEL):
        tall = min(2 * PANEL, BLOCK - start)
        row_id = lax.broadcasted_iota(jnp.int32, (tall, BLOCK), 0)
        left = work_ref[start : start + tall, :BLOCK]
        right = work_ref[start : start + tall, BLOCK:]
        cols = [
            jnp.broadcast_to(left[:, start + j : start + j + 1], (tall, BLOCK))
            for j in range(PANEL)
        ]
        for j in range(PANEL):
            root = lax.rsqrt(cols[j][j : j + 1, :])
            scaled = cols[j] * root
            for later in range(j + 1, PANEL):
                cols[later] = cols[later] - scaled * (cols[later][j : j + 1, :] * root)
            left_row = left[j : j + 1, :] * root
            right_row = right[j : j + 1, :] * root
            below = jnp.where(row_id > j, scaled, 0.0)
            left = jnp.where(row_id == j, left_row, left - below * left_row)
            right = jnp.where(row_id == j, right_row, right - below * right_row)
        work_ref[start : start + tall, :BLOCK] = left
        work_ref[start : start + tall, BLOCK:] = right
        rest = start + tall
        if rest < BLOCK:
            left, right = left[:PANEL], right[:PANEL]
            update = dot3_t(left, jnp.concatenate([left, right], axis=1))
            work_ref[rest:, :] = work_ref[rest:, :] - update[rest:, :]


def factor_kernel(
    scale, gram_ref, features_hbm, upper_ref, leverage_ref,
    state_ref, work_ref, right_ref, features_ref, copy_sem,
):
    columns = gram_ref.shape[0]
    count = columns // BLOCK
    fetch = pltpu.make_async_copy(features_hbm, features_ref, copy_sem)
    fetch.start()
    state_ref[...] = gram_ref[...]
    row_id = lax.broadcasted_iota(jnp.int32, (BLOCK, BLOCK), 0)
    col_id = lax.broadcasted_iota(jnp.int32, (BLOCK, BLOCK), 1)
    wide_id = lax.broadcasted_iota(jnp.int32, (BLOCK, columns), 1)

    def outer(k, carry):
        here = pl.multiple_of(k * BLOCK, BLOCK)
        rows = pl.ds(here, BLOCK)
        work_ref[:, :BLOCK] = state_ref[rows, rows]
        work_ref[:, BLOCK:] = jnp.where(row_id == col_id, 1.0, 0.0)
        factor_block(work_ref)
        inverse = jnp.where(col_id <= row_id, work_ref[:, BLOCK:], 0.0)
        panel = dot3(inverse, state_ref[rows, :])
        upper_ref[rows, :] = jnp.where(wide_id >= here + BLOCK, panel, 0.0)
        upper_ref[rows, rows] = jnp.where(col_id >= row_id, work_ref[:, :BLOCK], 0.0)
        state_ref[rows, :] = panel
        state_ref[rows, rows] = inverse
        high, low = halves(state_ref[rows, :])
        right_ref[...] = jnp.concatenate([high, low, high], axis=0).astype(BF16)

        def trailing(i, carry):
            below = pl.ds(pl.multiple_of(i * BLOCK, BLOCK), BLOCK)
            part = upper_ref[rows, below].T
            p_high, p_low = halves(part)
            left = jnp.concatenate([p_high, p_high, p_low], axis=1).astype(BF16)
            state_ref[below, rows] = jnp.zeros((BLOCK, BLOCK), F32)
            state_ref[below, :] = state_ref[below, :] - jnp.dot(
                left, right_ref[...], preferred_element_type=F32
            )
            return carry

        return lax.fori_loop(k + 1, count, trailing, carry)

    lax.fori_loop(0, count, outer, 0)
    fetch.wait()
    total = jnp.zeros((1, features_ref.shape[0]), F32)
    tile = 2 * BLOCK
    for start in range(0, columns, tile):
        depth = start + tile
        block = state_ref[start:depth, :depth]
        keep = (
            lax.broadcasted_iota(jnp.int32, (tile, depth), 1)
            <= lax.broadcasted_iota(jnp.int32, (tile, depth), 0) + start
        )
        high, low = halves(jnp.where(keep, block, 0.0))
        stacked = jnp.concatenate([high, low], axis=0).astype(BF16)
        solved = lax.dot_general(
            stacked,
            features_ref[:, :depth],
            (((1,), (1,)), ((), ())),
            preferred_element_type=F32,
        )
        solved = solved[:tile] + solved[tile:]
        total = total + jnp.sum(solved * solved, axis=0, keepdims=True)
    leverage_ref[...] = total * scale


def factor_return_kernel(
    scale, gram_ref, features_hbm, picked_ref, upper_ref, leverage_ref, sketch_ref,
    state_ref, work_ref, right_ref, features_ref, copy_sem, returned, row_send, row_recv,
):
    me = lax.axis_index("rows")
    size, most = picked_ref.shape[:2]
    greet_all(me, size)
    await_all(size)

    def row_copy(step):
        offset = 1 + lax.rem(size // 2 - 1 + step, size - 1)
        owner = lax.rem(me + offset, size)
        return pltpu.make_async_remote_copy(
            src_ref=picked_ref.at[owner],
            dst_ref=returned.at[me],
            send_sem=row_send.at[offset],
            recv_sem=row_recv.at[offset],
            device_id=place_of(owner),
            device_id_type=pl.DeviceIdType.MESH,
        )

    def begin(step, carry):
        row_copy(step).start()
        return carry

    def finish(step, carry):
        row_copy(step).wait()
        return carry

    lax.fori_loop(0, size - 1, begin, 0)
    returned[me] = picked_ref[me]
    factor_kernel(
        scale, gram_ref, features_hbm, upper_ref, leverage_ref,
        state_ref, work_ref, right_ref, features_ref, copy_sem,
    )
    lax.fori_loop(0, size - 1, finish, 0)
    for group in range(size):
        sketch_ref[group * most : (group + 1) * most, :] = returned[group]


def factor(gram, features, scale, picked=None):
    columns = gram.shape[0]
    rows_dev = features.shape[0]
    vmem = pl.BlockSpec(memory_space=pltpu.VMEM)
    kernel, inputs, more, own = factor_kernel, (gram, features), [], {}
    outputs = [
        jax.ShapeDtypeStruct((columns, columns), F32),
        jax.ShapeDtypeStruct((1, rows_dev), F32),
    ]
    if picked is not None:
        size, most = picked.shape[:2]
        kernel, inputs = factor_return_kernel, (gram, features, picked)
        outputs.append(jax.ShapeDtypeStruct((size * most, columns), F32))
        more = [
            pltpu.VMEM(picked.shape, F32),
            pltpu.SemaphoreType.DMA((size,)),
            pltpu.SemaphoreType.DMA((size,)),
        ]
        own = {"collective_id": 3, "has_side_effects": True}
    return pl.pallas_call(
        functools.partial(kernel, scale),
        out_shape=outputs,
        in_specs=[vmem, pl.BlockSpec(memory_space=pl.ANY), vmem][: len(inputs)],
        out_specs=[vmem] * len(outputs),
        scratch_shapes=[
            pltpu.VMEM((columns, columns), F32),
            pltpu.VMEM((BLOCK, 2 * BLOCK), F32),
            pltpu.VMEM((3 * BLOCK, columns), BF16),
            pltpu.VMEM(features.shape, BF16),
            pltpu.SemaphoreType.DMA,
        ]
        + more,
        compiler_params=pltpu.CompilerParams(vmem_limit_bytes=40 * 2**20, **own),
        cost_estimate=pl.CostEstimate(
            flops=20 * columns**3, bytes_accessed=16 * columns**2, transcendentals=0
        ),
        name="cholesky_leverage",
    )(*inputs)


def rank_in_group(group_of):
    count = group_of.shape[-1]
    same = group_of[:, None] == group_of[None, :]
    order = jnp.arange(count, dtype=jnp.int32)
    before = order[:, None] < order[None, :]
    return jnp.sum((same & before).astype(jnp.int32), axis=0)


def shards(features, flip_signs, sample_rows):
    rows_dev, columns = features.shape
    group_size = lax.axis_size("rows")
    position = lax.axis_index("rows")
    span = rows_dev // group_size
    samp_dev = sample_rows.shape[0]
    most = max(1, samp_dev // group_size)
    if span % 16 == 0:
        received, wanted = exchange(features, flip_signs, sample_rows, group_size)
    else:
        pieces = transform(features, flip_signs).reshape(group_size, span, columns)
        wanted = lax.all_gather(sample_rows, "rows", axis=0, tiled=True)
        wanted = wanted.reshape(group_size, samp_dev)
        received = lax.all_to_all(pieces, "rows", split_axis=0, concat_axis=0, tiled=True)
        received = received.reshape(1, rows_dev, columns)
    picked, packed = combine(wanted, received, position, most, span, rows_dev)
    own_scale = rows_dev * group_size / columns
    if (
        4 < group_size
        and columns // 2 % (16 * group_size) == 0
        and group_size * most == samp_dev
    ):
        gram_matrix = sum_over_devices(packed, group_size)
        upper_factor, leverage, sketch = factor(gram_matrix, features, own_scale, picked)
        return (sketch, upper_factor, leverage.reshape(rows_dev))
    gram_matrix = unpack_whole(lax.psum(packed, "rows"))
    gram_matrix, picked = lax.optimization_barrier((gram_matrix, picked))
    returned = lax.all_to_all(picked, "rows", split_axis=0, concat_axis=0, tiled=True)
    upper_factor, leverage = factor(gram_matrix, features, own_scale)
    own_groups = (sample_rows - position * rows_dev) // span
    own_ranks = rank_in_group(own_groups)
    sketch = jnp.take(
        returned.reshape(group_size * most, columns), own_groups * most + own_ranks, axis=0
    )
    return (sketch, upper_factor, leverage.reshape(rows_dev))


def solution(mesh):
    placed = (P("rows", None), P("rows"), P("rows"))
    return jax.shard_map(
        shards,
        mesh=mesh,
        in_specs=placed,
        out_specs=(P("rows", None), P(), P("rows")),
        check_vma=False,
    )
```

```python
import functools
import math

import jax
import jax.numpy as jnp
from jax import lax
from jax.experimental import pallas as pl
from jax.experimental.pallas import tpu as pltpu
from jax.sharding import PartitionSpec as P

FACTOR = 128
SAMPLES = 4096
BLOCK = 128
PANEL = 16
F32 = jnp.float32
BF16 = jnp.bfloat16


def hadamard_signs(rows, columns):
    bits = rows & columns
    shift = 16
    while shift >= 1:
        bits = bits ^ (bits >> shift)
        shift //= 2
    return (1 - 2 * (bits & 1)).astype(F32)


def halves(x):
    high = x.astype(BF16).astype(F32)
    return high, x - high


def dot3(a, b):
    a_high, a_low = halves(a)
    b_high, b_low = halves(b)
    left = jnp.concatenate([a_high, a_high, a_low], axis=1).astype(BF16)
    right = jnp.concatenate([b_high, b_low, b_high], axis=0).astype(BF16)
    return jnp.dot(left, right, preferred_element_type=F32)


def dot3_t(a, b):
    a_high, a_low = halves(a)
    b_high, b_low = halves(b)
    left = jnp.concatenate([a_high, a_high, a_low], axis=0).T.astype(BF16)
    right = jnp.concatenate([b_high, b_low, b_high], axis=0).astype(BF16)
    return jnp.dot(left, right, preferred_element_type=F32)


def transform_tile(signs_ref, features_ref, source, out_ref, target):
    groups = signs_ref.shape[0]
    table = hadamard_signs(
        lax.broadcasted_iota(jnp.int32, (FACTOR, FACTOR), 0),
        lax.broadcasted_iota(jnp.int32, (FACTOR, FACTOR), 1),
    )
    inner = []
    for b in range(groups):
        signed = (table * signs_ref[b : b + 1, :].astype(F32)).astype(BF16)
        rows = features_ref[b * FACTOR : (b + 1) * FACTOR, source]
        product = jnp.dot(signed, rows, preferred_element_type=F32)
        inner.append(product.astype(BF16).astype(F32))
    step = 1
    while step < groups:
        mixed = list(inner)
        for b in range(groups):
            if b & step == 0:
                mixed[b] = inner[b] + inner[b + step]
                mixed[b + step] = inner[b] - inner[b + step]
        inner = mixed
        step *= 2
    for b in range(groups):
        out_ref[b * FACTOR : (b + 1) * FACTOR, target] = inner[b].astype(BF16)


def transform_kernel(signs_ref, features_ref, out_ref):
    every = slice(None)
    transform_tile(signs_ref, features_ref, every, out_ref, every)


def transform(features, flip_signs):
    rows_dev, columns = features.shape
    tile = 128
    groups = rows_dev // FACTOR
    return pl.pallas_call(
        transform_kernel,
        grid=(columns // tile,),
        out_shape=jax.ShapeDtypeStruct((rows_dev, columns), BF16),
        in_specs=[
            pl.BlockSpec((groups, FACTOR), lambda i: (0, 0)),
            pl.BlockSpec((rows_dev, tile), lambda i: (0, i)),
        ],
        out_specs=pl.BlockSpec((rows_dev, tile), lambda i: (0, i)),
        compiler_params=pltpu.CompilerParams(vmem_limit_bytes=32 * 2**20),
        name="local_transform",
    )(flip_signs.reshape(groups, FACTOR), features)


def place_of(device):
    return {"rows": device}


def greet_all(me, size):
    barrier = pltpu.get_barrier_semaphore()

    def signal(offset, carry):
        pl.semaphore_signal(
            barrier,
            inc=1,
            device_id=place_of(lax.rem(me + offset, size)),
            device_id_type=pl.DeviceIdType.MESH,
        )
        return carry

    lax.fori_loop(1, size, signal, 0)


def await_all(size):
    pl.semaphore_wait(pltpu.get_barrier_semaphore(), size - 1)


def greet(partners):
    barrier = pltpu.get_barrier_semaphore()
    for partner in partners:
        pl.semaphore_signal(
            barrier, inc=1, device_id=place_of(partner), device_id_type=pl.DeviceIdType.MESH
        )
    pl.semaphore_wait(barrier, len(partners))


def exchange_kernel(
    signs_ref, features_ref, rows_ref, received_ref, wanted_ref,
    pieces, send, recv, row_send, row_recv,
):
    size = wanted_ref.shape[0]
    parts, rows_dev, part_columns = received_ref.shape
    span = rows_dev // size
    me = lax.axis_index("rows")
    greet_all(me, size)

    def slab(device):
        return pl.ds(pl.multiple_of(device * span, 16), span)

    def place(step):
        offset = 1 + lax.rem(size // 2 - 1 + step, size - 1)
        return offset, lax.rem(me + offset, size)

    def row_copy(step):
        offset, partner = place(step)
        return pltpu.make_async_remote_copy(
            src_ref=rows_ref.at[0],
            dst_ref=wanted_ref.at[me],
            send_sem=row_send.at[offset],
            recv_sem=row_recv.at[offset],
            device_id=place_of(partner),
            device_id_type=pl.DeviceIdType.MESH,
        )

    def data_copy(part, step):
        offset, partner = place(step)
        return pltpu.make_async_remote_copy(
            src_ref=pieces.at[part, slab(partner), :],
            dst_ref=received_ref.at[part, slab(me), :],
            send_sem=send.at[part, offset],
            recv_sem=recv.at[part, offset],
            device_id=place_of(partner),
            device_id_type=pl.DeviceIdType.MESH,
        )

    def begin_rows(step, carry):
        row_copy(step).start()
        return carry

    for part in range(parts):

        def tile(i, carry):
            source = pl.ds(pl.multiple_of(part * part_columns + i * FACTOR, FACTOR), FACTOR)
            target = pl.ds(pl.multiple_of(i * FACTOR, FACTOR), FACTOR)
            transform_tile(signs_ref, features_ref, source, pieces.at[part], target)
            return carry

        lax.fori_loop(0, part_columns // FACTOR, tile, 0)
        if part == 0:
            await_all(size)

        def begin(step, carry):
            data_copy(part, step).start()
            return carry

        lax.fori_loop(0, size - 1, begin, 0)
    lax.fori_loop(0, size - 1, begin_rows, 0)
    for part in range(parts):
        received_ref[part, slab(me), :] = pieces[part, slab(me), :]
    wanted_ref[me] = rows_ref[0]

    def finish(step, carry):
        for part in range(parts):
            data_copy(part, step).wait()
        row_copy(step).wait()
        return carry

    lax.fori_loop(0, size - 1, finish, 0)


def exchange(features, flip_signs, sample_rows, size):
    rows_dev, columns = features.shape
    groups = rows_dev // FACTOR
    samples = sample_rows.shape[0]
    parts = 2
    shape = (parts, rows_dev, columns // parts)
    vmem = pl.BlockSpec(memory_space=pltpu.VMEM)
    received, wanted = pl.pallas_call(
        exchange_kernel,
        out_shape=(
            jax.ShapeDtypeStruct(shape, BF16),
            jax.ShapeDtypeStruct((size, 1, samples), jnp.int32),
        ),
        in_specs=[vmem] * 3,
        out_specs=(vmem, vmem),
        scratch_shapes=[
            pltpu.VMEM(shape, BF16),
            pltpu.SemaphoreType.DMA((parts, size)),
            pltpu.SemaphoreType.DMA((parts, size)),
            pltpu.SemaphoreType.DMA((size,)),
            pltpu.SemaphoreType.DMA((size,)),
        ],
        compiler_params=pltpu.CompilerParams(
            collective_id=1, has_side_effects=True, vmem_limit_bytes=24 * 2**20
        ),
        name="transform_exchange",
    )(
        flip_signs.reshape(groups, FACTOR),
        features,
        sample_rows.reshape(1, 1, samples),
    )
    return received, wanted.reshape(size, samples)


def sum_kernel(orders, packed_ref, gram_ref, work, land, summed, send, recv):
    me = lax.axis_index("rows")
    stages = len(orders[0])
    span = packed_ref.shape[0] // len(orders)
    bit = [me // 2**b % 2 for b in range(stages)]
    partner = [me + (1 - 2 * bit[b]) * 2**b for b in range(stages)]
    greet(partner)

    def rows(start, size):
        return pl.ds(pl.multiple_of(start, 8), size)

    def reduce_part(part, order):
        start, size, landing = part * span, span, part * span
        kept = []
        for stage, b in enumerate(order):
            size //= 2
            source = packed_ref if stage == 0 else work
            kept_start = start + bit[b] * size
            copy = pltpu.make_async_remote_copy(
                src_ref=source.at[rows(start + (1 - bit[b]) * size, size), :],
                dst_ref=land.at[pl.ds(landing, size), :],
                send_sem=send.at[part, stage],
                recv_sem=recv.at[part, stage],
                device_id=place_of(partner[b]),
                device_id_type=pl.DeviceIdType.MESH,
            )
            copy.start()
            yield
            copy.wait()
            target = work if stage < stages - 1 else summed
            target[rows(kept_start, size), :] = (
                source[rows(kept_start, size), :] + land[pl.ds(landing, size), :]
            )
            landing += size
            start = kept_start
            kept.append((b, start, size))
        for stage, (b, start, size) in enumerate(reversed(kept)):
            block = summed.at[rows(start, size), :]
            copy = pltpu.make_async_remote_copy(
                src_ref=block,
                dst_ref=block,
                send_sem=send.at[part, stages + stage],
                recv_sem=recv.at[part, stages + stage],
                device_id=place_of(partner[b]),
                device_id_type=pl.DeviceIdType.MESH,
            )
            copy.start()
            yield
            copy.wait()

    parts = [reduce_part(part, order) for part, order in enumerate(orders)]
    done = object()
    while parts:
        parts = [part for part in parts if next(part, done) is not done]
    unpack(summed, gram_ref)


def blocks_of(columns):
    count = columns // BLOCK
    for i in range(count // 2):
        yield i, i, 0
        yield count - 1 - i, i, (count - i) * BLOCK


def unpack(packed_ref, gram_ref):
    columns = gram_ref.shape[0]
    for block, row, at in blocks_of(columns):
        width = columns - block * BLOCK
        gram_ref[block * BLOCK : (block + 1) * BLOCK, block * BLOCK :] = packed_ref[
            row * BLOCK : (row + 1) * BLOCK, at : at + width
        ]
        if block:
            gram_ref[block * BLOCK : (block + 1) * BLOCK, : block * BLOCK] = jnp.zeros(
                (BLOCK, block * BLOCK), F32
            )


def sum_over_devices(packed, size):
    rows, width = packed.shape
    columns = 2 * rows
    vmem = pl.BlockSpec(memory_space=pltpu.VMEM)
    bits = list(range(size.bit_length() - 1))
    other = list(bits)
    other[1], other[2] = bits[2], bits[1]
    other[3:5] = reversed(bits[3:5])
    return pl.pallas_call(
        functools.partial(sum_kernel, (bits, other)),
        out_shape=jax.ShapeDtypeStruct((columns, columns), F32),
        in_specs=[vmem],
        out_specs=vmem,
        scratch_shapes=[
            pltpu.VMEM((rows, width), F32),
            pltpu.VMEM((rows, width), F32),
            pltpu.VMEM((rows, width), F32),
            pltpu.SemaphoreType.DMA((2, 2 * len(bits))),
            pltpu.SemaphoreType.DMA((2, 2 * len(bits))),
        ],
        compiler_params=pltpu.CompilerParams(
            collective_id=2, has_side_effects=True, vmem_limit_bytes=24 * 2**20
        ),
        name="sum_grams",
    )(packed)


def unpack_whole(packed):
    columns = 2 * packed.shape[0]
    gram = jnp.zeros((columns, columns), F32)
    for block, row, at in blocks_of(columns):
        width = columns - block * BLOCK
        part = packed[row * BLOCK : (row + 1) * BLOCK, at : at + width]
        gram = lax.dynamic_update_slice(gram, part, (block * BLOCK, block * BLOCK))
    return gram


def combine_kernel(most, span, rows_dev, position_ref, wanted_ref, received_ref, picked_ref, packed_ref):
    slots, samples = wanted_ref.shape
    total = received_ref.shape[1]
    position = position_ref[0]
    row_id = lax.broadcasted_iota(jnp.int32, (slots, samples), 0)
    inside = wanted_ref[...] - row_id // most * rows_dev - position * span
    mine = (inside >= 0) & (inside < span)
    earlier = (
        lax.broadcasted_iota(jnp.int32, (samples, samples), 0)
        < lax.broadcasted_iota(jnp.int32, (samples, samples), 1)
    )
    rank = jnp.dot(
        jnp.where(mine, 1.0, 0.0).astype(BF16),
        jnp.where(earlier, 1.0, 0.0).astype(BF16),
        preferred_element_type=F32,
    )
    hit = mine & (rank == (row_id % most).astype(F32))
    place = jnp.max(jnp.where(hit, inside, -1), axis=1, keepdims=True)
    to_block = lax.broadcasted_iota(jnp.int32, (slots, total), 0) // most
    column = lax.broadcasted_iota(jnp.int32, (slots, total), 1)
    sign = hadamard_signs(to_block, column // span)
    choose = jnp.where(column % span == place, sign, 0.0).astype(BF16)
    picked = jnp.concatenate(
        [
            jnp.dot(choose, received_ref[part], preferred_element_type=F32)
            for part in range(received_ref.shape[0])
        ],
        axis=1,
    )
    picked = picked * (1.0 / math.sqrt(SAMPLES))
    for group in range(slots // most):
        picked_ref[group] = picked[group * most : (group + 1) * most, :]
    high, low = halves(picked)
    left = jnp.concatenate([high, high, low], axis=0).T.astype(BF16)
    right = jnp.concatenate([high, low, high], axis=0).astype(BF16)
    columns = picked.shape[1]
    for block, row, at in blocks_of(columns):
        start = block * BLOCK
        packed_ref[row * BLOCK : (row + 1) * BLOCK, at : at + columns - start] = jnp.dot(
            left[start : start + BLOCK, :], right[:, start:], preferred_element_type=F32
        )


def combine(wanted, received, position, most, span, rows_dev):
    slots = wanted.shape[0] * most
    columns = received.shape[0] * received.shape[2]
    repeated = jnp.repeat(wanted, most, axis=0)
    vmem = pl.BlockSpec(memory_space=pltpu.VMEM)
    return pl.pallas_call(
        functools.partial(combine_kernel, most, span, rows_dev),
        out_shape=(
            jax.ShapeDtypeStruct((wanted.shape[0], most, columns), F32),
            jax.ShapeDtypeStruct((columns // 2, columns + BLOCK), F32),
        ),
        in_specs=[pl.BlockSpec(memory_space=pltpu.SMEM), vmem, vmem],
        out_specs=(vmem, vmem),
        compiler_params=pltpu.CompilerParams(vmem_limit_bytes=32 * 2**20),
        name="combine_pick_gram",
    )(position.reshape(1), repeated, received)


def factor_block(work_ref):
    for start in range(0, BLOCK, PANEL):
        tall = min(2 * PANEL, BLOCK - start)
        row_id = lax.broadcasted_iota(jnp.int32, (tall, BLOCK), 0)
        left = work_ref[start : start + tall, :BLOCK]
        right = work_ref[start : start + tall, BLOCK:]
        cols = [
            jnp.broadcast_to(left[:, start + j : start + j + 1], (tall, BLOCK))
            for j in range(PANEL)
        ]
        for j in range(PANEL):
            root = lax.rsqrt(cols[j][j : j + 1, :])
            scaled = cols[j] * root
            for later in range(j + 1, PANEL):
                cols[later] = cols[later] - scaled * (cols[later][j : j + 1, :] * root)
            left_row = left[j : j + 1, :] * root
            right_row = right[j : j + 1, :] * root
            below = jnp.where(row_id > j, scaled, 0.0)
            left = jnp.where(row_id == j, left_row, left - below * left_row)
            right = jnp.where(row_id == j, right_row, right - below * right_row)
        work_ref[start : start + tall, :BLOCK] = left
        work_ref[start : start + tall, BLOCK:] = right
        rest = start + tall
        if rest < BLOCK:
            left, right = left[:PANEL], right[:PANEL]
            update = dot3_t(left, jnp.concatenate([left, right], axis=1))
            work_ref[rest:, :] = work_ref[rest:, :] - update[rest:, :]


def factor_kernel(
    scale, gram_ref, features_hbm, upper_ref, leverage_ref,
    state_ref, work_ref, right_ref, features_ref, copy_sem,
):
    columns = gram_ref.shape[0]
    count = columns // BLOCK
    fetch = pltpu.make_async_copy(features_hbm, features_ref, copy_sem)
    fetch.start()
    state_ref[...] = gram_ref[...]
    row_id = lax.broadcasted_iota(jnp.int32, (BLOCK, BLOCK), 0)
    col_id = lax.broadcasted_iota(jnp.int32, (BLOCK, BLOCK), 1)
    wide_id = lax.broadcasted_iota(jnp.int32, (BLOCK, columns), 1)

    def outer(k, carry):
        here = pl.multiple_of(k * BLOCK, BLOCK)
        rows = pl.ds(here, BLOCK)
        work_ref[:, :BLOCK] = state_ref[rows, rows]
        work_ref[:, BLOCK:] = jnp.where(row_id == col_id, 1.0, 0.0)
        factor_block(work_ref)
        inverse = jnp.where(col_id <= row_id, work_ref[:, BLOCK:], 0.0)
        panel = dot3(inverse, state_ref[rows, :])
        upper_ref[rows, :] = jnp.where(wide_id >= here + BLOCK, panel, 0.0)
        upper_ref[rows, rows] = jnp.where(col_id >= row_id, work_ref[:, :BLOCK], 0.0)
        state_ref[rows, :] = panel
        state_ref[rows, rows] = inverse
        high, low = halves(state_ref[rows, :])
        right_ref[...] = jnp.concatenate([high, low, high], axis=0).astype(BF16)

        def trailing(i, carry):
            below = pl.ds(pl.multiple_of(i * BLOCK, BLOCK), BLOCK)
            part = upper_ref[rows, below].T
            p_high, p_low = halves(part)
            left = jnp.concatenate([p_high, p_high, p_low], axis=1).astype(BF16)
            state_ref[below, rows] = jnp.zeros((BLOCK, BLOCK), F32)
            state_ref[below, :] = state_ref[below, :] - jnp.dot(
                left, right_ref[...], preferred_element_type=F32
            )
            return carry

        return lax.fori_loop(k + 1, count, trailing, carry)

    lax.fori_loop(0, count, outer, 0)
    fetch.wait()
    total = jnp.zeros((1, features_ref.shape[0]), F32)
    tile = 2 * BLOCK
    for start in range(0, columns, tile):
        depth = start + tile
        block = state_ref[start:depth, :depth]
        keep = (
            lax.broadcasted_iota(jnp.int32, (tile, depth), 1)
            <= lax.broadcasted_iota(jnp.int32, (tile, depth), 0) + start
        )
        high, low = halves(jnp.where(keep, block, 0.0))
        stacked = jnp.concatenate([high, low], axis=0).astype(BF16)
        solved = lax.dot_general(
            stacked,
            features_ref[:, :depth],
            (((1,), (1,)), ((), ())),
            preferred_element_type=F32,
        )
        solved = solved[:tile] + solved[tile:]
        total = total + jnp.sum(solved * solved, axis=0, keepdims=True)
    leverage_ref[...] = total * scale


def factor_return_kernel(
    scale, gram_ref, features_hbm, picked_ref, upper_ref, leverage_ref, sketch_ref,
    state_ref, work_ref, right_ref, features_ref, copy_sem, returned, row_send, row_recv,
):
    me = lax.axis_index("rows")
    size, most = picked_ref.shape[:2]
    greet_all(me, size)
    await_all(size)

    def row_copy(step):
        offset = 1 + lax.rem(size // 2 - 1 + step, size - 1)
        owner = lax.rem(me + offset, size)
        return pltpu.make_async_remote_copy(
            src_ref=picked_ref.at[owner],
            dst_ref=returned.at[me],
            send_sem=row_send.at[offset],
            recv_sem=row_recv.at[offset],
            device_id=place_of(owner),
            device_id_type=pl.DeviceIdType.MESH,
        )

    def begin(step, carry):
        row_copy(step).start()
        return carry

    def finish(step, carry):
        row_copy(step).wait()
        return carry

    lax.fori_loop(0, size - 1, begin, 0)
    returned[me] = picked_ref[me]
    factor_kernel(
        scale, gram_ref, features_hbm, upper_ref, leverage_ref,
        state_ref, work_ref, right_ref, features_ref, copy_sem,
    )
    lax.fori_loop(0, size - 1, finish, 0)
    for group in range(size):
        sketch_ref[group * most : (group + 1) * most, :] = returned[group]


def factor(gram, features, scale, picked=None):
    columns = gram.shape[0]
    rows_dev = features.shape[0]
    vmem = pl.BlockSpec(memory_space=pltpu.VMEM)
    kernel, inputs, more, own = factor_kernel, (gram, features), [], {}
    outputs = [
        jax.ShapeDtypeStruct((columns, columns), F32),
        jax.ShapeDtypeStruct((1, rows_dev), F32),
    ]
    if picked is not None:
        size, most = picked.shape[:2]
        kernel, inputs = factor_return_kernel, (gram, features, picked)
        outputs.append(jax.ShapeDtypeStruct((size * most, columns), F32))
        more = [
            pltpu.VMEM(picked.shape, F32),
            pltpu.SemaphoreType.DMA((size,)),
            pltpu.SemaphoreType.DMA((size,)),
        ]
        own = {"collective_id": 3, "has_side_effects": True}
    return pl.pallas_call(
        functools.partial(kernel, scale),
        out_shape=outputs,
        in_specs=[vmem, pl.BlockSpec(memory_space=pl.ANY), vmem][: len(inputs)],
        out_specs=[vmem] * len(outputs),
        scratch_shapes=[
            pltpu.VMEM((columns, columns), F32),
            pltpu.VMEM((BLOCK, 2 * BLOCK), F32),
            pltpu.VMEM((3 * BLOCK, columns), BF16),
            pltpu.VMEM(features.shape, BF16),
            pltpu.SemaphoreType.DMA,
        ]
        + more,
        compiler_params=pltpu.CompilerParams(vmem_limit_bytes=40 * 2**20, **own),
        cost_estimate=pl.CostEstimate(
            flops=20 * columns**3, bytes_accessed=16 * columns**2, transcendentals=0
        ),
        name="cholesky_leverage",
    )(*inputs)


def rank_in_group(group_of):
    count = group_of.shape[-1]
    same = group_of[:, None] == group_of[None, :]
    order = jnp.arange(count, dtype=jnp.int32)
    before = order[:, None] < order[None, :]
    return jnp.sum((same & before).astype(jnp.int32), axis=0)


def shards(features, flip_signs, sample_rows):
    rows_dev, columns = features.shape
    group_size = lax.axis_size("rows")
    position = lax.axis_index("rows")
    span = rows_dev // group_size
    samp_dev = sample_rows.shape[0]
    most = max(1, samp_dev // group_size)
    if span % 16 == 0:
        received, wanted = exchange(features, flip_signs, sample_rows, group_size)
    else:
        pieces = transform(features, flip_signs).reshape(group_size, span, columns)
        wanted = lax.all_gather(sample_rows, "rows", axis=0, tiled=True)
        wanted = wanted.reshape(group_size, samp_dev)
        received = lax.all_to_all(pieces, "rows", split_axis=0, concat_axis=0, tiled=True)
        received = received.reshape(1, rows_dev, columns)
    picked, packed = combine(wanted, received, position, most, span, rows_dev)
    own_scale = rows_dev * group_size / columns
    if (
        4 < group_size
        and columns // 2 % (16 * group_size) == 0
        and group_size * most == samp_dev
    ):
        gram_matrix = sum_over_devices(packed, group_size)
        upper_factor, leverage, sketch = factor(gram_matrix, features, own_scale, picked)
        return (sketch, upper_factor, leverage.reshape(rows_dev))
    gram_matrix = unpack_whole(lax.psum(packed, "rows"))
    gram_matrix, picked = lax.optimization_barrier((gram_matrix, picked))
    returned = lax.all_to_all(picked, "rows", split_axis=0, concat_axis=0, tiled=True)
    upper_factor, leverage = factor(gram_matrix, features, own_scale)
    own_groups = (sample_rows - position * rows_dev) // span
    own_ranks = rank_in_group(own_groups)
    sketch = jnp.take(
        returned.reshape(group_size * most, columns), own_groups * most + own_ranks, axis=0
    )
    return (sketch, upper_factor, leverage.reshape(rows_dev))


def solution(mesh):
    placed = (P("rows", None), P("rows"), P("rows"))
    return jax.shard_map(
        shards,
        mesh=mesh,
        in_specs=placed,
        out_specs=(P("rows", None), P(), P("rows")),
        check_vma=False,
    )
```
